32 devices in a mesh: seq: 8 (over z, y), tp: 4 (over x, core).
Axes of the slice: x: 2, y: 2, z: 4, core: 2. Of those that a mesh axis runs over, the one named last changes fastest.
Arguments:
- stream_in: bfloat16 [1024, 2880], P('seq'), may hold values from -40 to 40
- attn_gain: float32 [2880], replicated, may hold values from 0.1 to 1.9
- w_qkv: bfloat16 [2880, 8, 640], P(None, 'tp'), may hold values from -2 to 2
- key_value_cache: bfloat16 [128, 8, 128], P(None, 'tp'), may hold values from -6 to 6
- w_out: bfloat16 [4096, 2880], P('tp'), may hold values from -0.09375 to 0.09375
- mlp_gain: float32 [2880], replicated, may hold values from 0.1 to 1.9
- expert_index: int32 [1024, 4], P(('seq', 'tp')), may hold values from 0 to 31, all different within a row; in each aligned block of 32 rows (0 to 31, 32 to 63, ...) at most 8 rows name the same one
- gate_weight: float32 [1024, 4], P(('seq', 'tp')), may hold values from 0.05 to 0.5
- w_gateup: bfloat16 [32, 2880, 2, 2880], P('seq', None, None, 'tp'), may hold values from -0.109375 to 0.109375
- w_down: bfloat16 [32, 2880, 2880], P('seq', 'tp'), may hold values from -0.109375 to 0.109375
Outputs:
- stream_out: bfloat16 [1024, 2880], P(('seq', 'tp'))
The draws below stay inside these ranges and needn't reach their ends.
Inputs may be any that keep to these rules, and one draw needn't show every extreme that they name: `expert_index`: in the rows of one device (aligned blocks of 32 rows) no expert is named by more than 8 rows, a bound that some block reaches; a row names 4 different experts.
All inputs are finite; a program needn't handle non-finite values.
Results may differ from the reference program's by a relative error of at most 0.01.
Values may be sent and summed in bfloat16 or wider, within the bound.
No kernel may reach another device: no remote copies, remote signals or barrier semaphores. Data moves between devices by JAX's collectives and lax.ppermute only.
A program may use at most 128 MiB of HBM per device.

```python
import math
import jax
import jax.numpy as jnp
import numpy as np
from jax import lax

MODEL_WIDTH = 2880
QUERY_HEADS = 64
KEY_VALUE_HEADS = 8
HEAD_SIZE = 64
WINDOW_KEYS = 128
EXPERTS = 32
FFE = 2880
TOPK = 4
TOK_DEV = 128
BLOCK_TOKENS = 1024
CAP = 8
N_SEQ = 8
N_TP = 4


def draw_stream_in(key, part):
    root_random_key = jax.random.fold_in(jax.random.fold_in(key, 11), 0)
    values = jax.random.normal(root_random_key, (BLOCK_TOKENS, MODEL_WIDTH), jnp.float32)
    return jnp.clip(values, -40.0, 40.0).astype(jnp.bfloat16)


def draw_w_qkv(key, part):
    root_random_key = jax.random.fold_in(jax.random.fold_in(key, 23), 0)
    query_group_width = QUERY_HEADS // KEY_VALUE_HEADS
    layer_weights = jax.random.normal(root_random_key, (MODEL_WIDTH, KEY_VALUE_HEADS, query_group_width + 2, HEAD_SIZE), jnp.float32) * MODEL_WIDTH ** (-0.5)
    layer_weights = jnp.clip(layer_weights, -2.0, 2.0)
    return layer_weights.reshape(MODEL_WIDTH, KEY_VALUE_HEADS, (query_group_width + 2) * HEAD_SIZE).astype(jnp.bfloat16)


def levels(key, shape, pieces, smallest, high):
    def one(dim, shards_of):
        steps = jax.random.uniform(jax.random.fold_in(jax.random.fold_in(key, 6), dim), (shards_of,), jnp.float32, smallest / len(pieces), high / len(pieces))
        return jnp.repeat(jnp.exp(steps), shape[dim] // shards_of).reshape((-1,) + (1,) * (len(shape) - dim - 1))

    loudness = one(*pieces[0])
    for cut in pieces[1:]:
        loudness = loudness * one(*cut)
    return loudness


def assign_block(stream_key, own, number, rows, count, top, reach, slope):
    sequence = jax.random.permutation(stream_key, count)
    packed, common = portions_of(count, rows * top, reach, slope, True), portions_of(count, rows * top, reach, slope, False)
    places = jnp.arange(count)

    def named(sizes, turn):
        used = int((sizes > 0).sum())
        fixed = max(1, used // 4)
        passed = fixed + (places - fixed + turn * (used - fixed)) % max(1, count - fixed)
        return jnp.zeros((count,), jnp.int32).at[sequence[jnp.where(places < fixed, places, passed)]].set(jnp.asarray(sizes, jnp.int32))

    sizes = jnp.where(number % 4 == 0, named(packed, number // 4), named(common, number - number // 4 - 1))
    mixed = jax.random.permutation(jax.random.fold_in(own, 3), count)
    source_of, taker = mixed[0:count // 2 * 2:2], mixed[1:count // 2 * 2:2]
    slack = jnp.minimum(sizes[source_of] - 1, reach - sizes[taker]) // 2
    slack = jnp.where((source_of == sequence[0]) | (taker == sequence[0]) | (sizes[taker] == 0), 0, jnp.maximum(slack, 0))
    passed = jax.random.randint(jax.random.fold_in(own, 4), (count // 2,), 0, 1 << 20) % (slack + 1)
    sizes = sizes.at[source_of].add(-passed).at[taker].add(passed)
    items = jnp.searchsorted(jnp.cumsum(sizes), jnp.arange(rows * top), side="right").astype(jnp.int32)
    grid = items.reshape(top, rows).T
    grid = grid[jax.random.permutation(jax.random.fold_in(own, 1), rows)]
    turn = jax.random.randint(jax.random.fold_in(own, 2), (rows, 1), 0, top)
    return jnp.take_along_axis(grid, (jnp.arange(top)[None, :] + turn) % top, axis=1)


def portions_of(count, total, bound, skew, full):
    weights = [(1 << 20) // math.isqrt(standing ** skew) + 1 for standing in range(1, count + 1)]
    largest = bound if full else min(bound, max(-(-total // count), total * weights[0] // sum(weights)))
    least = 1 if total - largest >= count - 1 else 0
    holding, surplus = [largest] + [least] * (count - 1), total - largest - least * (count - 1)
    while surplus > 0:
        movable = [i for i in range(1, count) if holding[i] < largest] or [i for i in range(1, count) if holding[i] < bound]
        pool, remaining = sum([weights[i] for i in movable]), surplus
        for i in movable:
            addition = min(bound - holding[i], max(1, remaining * weights[i] // pool), surplus)
            holding[i] = holding[i] + addition
            surplus = surplus - addition
    return np.array(holding)


def bell_draw(stream_key, dims, spread, most, pieces=(), kind=jnp.bfloat16):
    entries = spread * jax.random.normal(stream_key, dims, jnp.float32)
    if pieces:
        entries = entries * levels(stream_key, dims, pieces, -0.22, 0.18)
    return jnp.clip(entries, -most, most).astype(kind)


def setup_inputs(seed: int = 0) -> dict:
    key_list = jax.random.split(jax.random.key(seed), 11)
    stream_in = draw_stream_in(jax.random.fold_in(key_list[10], 71), 0)
    attn_gain = jnp.clip(1.0 + 0.18 * jax.random.normal(key_list[1], (MODEL_WIDTH,), jnp.float32), 0.1, 1.9)
    w_qkv = draw_w_qkv(jax.random.fold_in(key_list[10], 71), 0)
    key_value_cache = bell_draw(key_list[3], (WINDOW_KEYS, KEY_VALUE_HEADS, 2 * HEAD_SIZE), 1.0, 6.0, ((1, 4),))
    w_out = bell_draw(key_list[4], (QUERY_HEADS * HEAD_SIZE, MODEL_WIDTH), (QUERY_HEADS * HEAD_SIZE) ** -0.5, 0.09375, ((0, 4),))
    mlp_gain = jnp.clip(1.0 + 0.18 * jax.random.normal(key_list[5], (MODEL_WIDTH,), jnp.float32), 0.1, 1.9)
    expert_index_keys = jax.random.split(jax.random.fold_in(key_list[6], 1), BLOCK_TOKENS // (TOK_DEV // N_TP))
    expert_index_turns = jax.random.permutation(jax.random.fold_in(key_list[6], 3), BLOCK_TOKENS // (TOK_DEV // N_TP))
    expert_index = jax.vmap(lambda own, number: assign_block(jax.random.fold_in(key_list[6], 2), own, number, TOK_DEV // N_TP, EXPERTS, TOPK, CAP, 2))(expert_index_keys, expert_index_turns).reshape((BLOCK_TOKENS, TOPK))
    gate_weight = jnp.clip(0.05 + 0.45 * jax.random.uniform(key_list[7], (BLOCK_TOKENS, TOPK), jnp.float32) ** levels(key_list[7], (BLOCK_TOKENS, TOPK), ((0, 32),), -0.2, 0.2), 0.05, 0.5)
    w_gateup = bell_draw(key_list[8], (EXPERTS, MODEL_WIDTH, 2, FFE), MODEL_WIDTH ** -0.5, 0.109375, ((0, 8), (3, 4)))
    w_down = bell_draw(key_list[9], (EXPERTS, FFE, MODEL_WIDTH), FFE ** -0.5, 0.109375, ((0, 8), (1, 4)))
    return {"stream_in": stream_in, "attn_gain": attn_gain, "w_qkv": w_qkv, "key_value_cache": key_value_cache, "w_out": w_out, "mlp_gain": mlp_gain, "expert_index": expert_index, "gate_weight": gate_weight, "w_gateup": w_gateup, "w_down": w_down}


EPS = 1e-05

def rms_scale(values, gain_vec):
    mean_sq = lax.optimization_barrier(jnp.mean(values * values, axis=-1, keepdims=True))
    return values * lax.rsqrt(mean_sq + EPS) * gain_vec

def window_block(queries, key_rows, value_rows):
    scores = jnp.einsum('qhgc,khc->hgqk', queries.astype(jnp.float32), key_rows.astype(jnp.float32)) * HEAD_SIZE ** (-0.5)
    key_offset = jnp.arange(key_rows.shape[0])[None, :] - jnp.arange(queries.shape[0])[:, None]
    in_window = (key_offset >= 1) & (key_offset <= WINDOW_KEYS)
    scores = jnp.where(in_window, scores, -1e+30)
    row_max = lax.optimization_barrier(jnp.max(scores, axis=-1, keepdims=True))
    exponent = jnp.exp(scores - row_max)
    layer_weights = (exponent / lax.optimization_barrier(jnp.sum(exponent, axis=-1, keepdims=True))).astype(jnp.bfloat16)
    attended = jnp.einsum('hgqk,khc->qhgc', layer_weights.astype(jnp.float32), value_rows.astype(jnp.float32))
    return attended.astype(jnp.bfloat16)

def reference(stream_in, attn_gain, w_qkv, key_value_cache, w_out, mlp_gain, expert_index, gate_weight, w_gateup, w_down):
    query_group_width = QUERY_HEADS // KEY_VALUE_HEADS
    normed = rms_scale(stream_in.astype(jnp.float32), attn_gain).astype(jnp.bfloat16)
    projected_rows = jnp.einsum('td,dhc->thc', normed.astype(jnp.float32), w_qkv.astype(jnp.float32)).astype(jnp.bfloat16)
    projected_rows = projected_rows.reshape(BLOCK_TOKENS, KEY_VALUE_HEADS, query_group_width + 2, HEAD_SIZE)
    queries = projected_rows[:, :, :query_group_width]
    key_rows = jnp.concatenate([key_value_cache[:, :, :HEAD_SIZE], projected_rows[:, :, query_group_width]], axis=0)
    value_rows = jnp.concatenate([key_value_cache[:, :, HEAD_SIZE:], projected_rows[:, :, query_group_width + 1]], axis=0)

    def one_block(block_index):
        row_start = (block_index * TOK_DEV).astype(jnp.int32)
        block_q = lax.dynamic_slice_in_dim(queries, row_start, TOK_DEV, 0)
        block_k = lax.dynamic_slice_in_dim(key_rows, row_start, TOK_DEV + WINDOW_KEYS, 0)
        block_v = lax.dynamic_slice_in_dim(value_rows, row_start, TOK_DEV + WINDOW_KEYS, 0)
        return window_block(block_q, block_k, block_v)
    attended = lax.map(one_block, jnp.arange(N_SEQ, dtype=jnp.int32)).reshape(BLOCK_TOKENS, QUERY_HEADS * HEAD_SIZE)
    residual = stream_in.astype(jnp.float32) + jnp.dot(attended, w_out, preferred_element_type=jnp.float32)
    hidden_in = rms_scale(residual, mlp_gain).astype(jnp.bfloat16)
    block_rows = TOK_DEV // N_TP
    blocks = BLOCK_TOKENS // block_rows
    capacity = 2 * TOK_DEV * TOPK // (N_TP * EXPERTS)
    flat_index = expert_index.reshape(blocks, block_rows * TOPK)
    onehot = (flat_index[:, :, None] == jnp.arange(EXPERTS, dtype=jnp.int32)[None, None, :]).astype(jnp.int32)
    slot_rank = lax.optimization_barrier(jnp.sum((jnp.cumsum(onehot, axis=1) - 1) * onehot, axis=2)).astype(jnp.int32)
    block_id = jnp.broadcast_to(jnp.arange(blocks, dtype=jnp.int32)[:, None], flat_index.shape)
    row_values = jnp.repeat(hidden_in.reshape(blocks, block_rows, MODEL_WIDTH), TOPK, axis=1)
    buffer = jnp.zeros((blocks, EXPERTS, capacity, MODEL_WIDTH), jnp.bfloat16).at[block_id, flat_index, slot_rank].set(row_values)
    slice_units = FFE // N_TP

    def one_expert(operands):
        chosen, gate_up_matrix, down_proj = operands
        input_rows = chosen.reshape(blocks * capacity, MODEL_WIDTH).astype(jnp.float32)
        gate_up_rows = jnp.einsum('vi,ipk->vpk', input_rows, gate_up_matrix.astype(jnp.float32))
        activated = (jax.nn.silu(gate_up_rows[:, 0]) * gate_up_rows[:, 1]).astype(jnp.bfloat16)
        partials = jnp.einsum('ltf,tfd->ltd', activated.reshape(-1, N_TP, slice_units).astype(jnp.float32), down_proj.reshape(N_TP, slice_units, MODEL_WIDTH).astype(jnp.float32))
        rounded = lax.optimization_barrier(partials.astype(jnp.bfloat16))
        total = lax.optimization_barrier(jnp.sum(rounded.astype(jnp.float32), axis=1))
        return total.astype(jnp.bfloat16).reshape(blocks, capacity, MODEL_WIDTH)
    results = lax.map(one_expert, (jnp.moveaxis(buffer, 1, 0), w_gateup, w_down))
    expert_out = results[flat_index, block_id, slot_rank].reshape(BLOCK_TOKENS, TOPK, MODEL_WIDTH)
    mixture = lax.optimization_barrier(jnp.sum(gate_weight[:, :, None] * expert_out.astype(jnp.float32), axis=1))
    return (residual + mixture).astype(jnp.bfloat16)
```

```python
import jax
import jax.numpy as jnp
from jax import lax
from jax.sharding import PartitionSpec as P

MODEL_WIDTH = 2880
QUERY_HEADS = 64
KEY_VALUE_HEADS = 8
HEAD_SIZE = 64
WINDOW_KEYS = 128
EXPERTS = 32
TOPK = 4


EPS = 1e-05


def from_behind(value, axis, steps):
    count = lax.axis_size(axis)
    first, last = (max(0, -steps), min(count, count - steps))
    return lax.ppermute(value, axis, [(source, source + steps) for source in range(first, last)])


def rms_scale(values, gain_vec):
    mean_sq = jnp.mean(values * values, axis=-1, keepdims=True)
    return values * lax.rsqrt(mean_sq + EPS) * gain_vec


def window_block(queries, key_rows, value_rows):
    scores = jnp.einsum(
        "qhgc,khc->hgqk", queries, key_rows, preferred_element_type=jnp.float32
    ) * HEAD_SIZE ** (-0.5)
    key_offset = jnp.arange(key_rows.shape[0])[None, :] - jnp.arange(queries.shape[0])[:, None]
    in_window = (key_offset >= 1) & (key_offset <= WINDOW_KEYS)
    scores = jnp.where(in_window, scores, -1e30)
    row_max = jnp.max(scores, axis=-1, keepdims=True)
    exponent = jnp.exp(scores - row_max)
    layer_weights = (exponent / jnp.sum(exponent, axis=-1, keepdims=True)).astype(jnp.bfloat16)
    attended = jnp.einsum(
        "hgqk,khc->qhgc", layer_weights, value_rows, preferred_element_type=jnp.float32
    )
    return attended.astype(jnp.bfloat16)


def local(
    stream_in,
    attn_gain,
    w_qkv,
    key_value_cache,
    w_out,
    mlp_gain,
    expert_index,
    gate_weight,
    w_gateup,
    w_down,
):
    seq_count = lax.axis_size("seq")
    tp_count = lax.axis_size("tp")
    length_local = stream_in.shape[0]
    heads_local = w_qkv.shape[1]
    query_group_width = QUERY_HEADS // KEY_VALUE_HEADS
    normed = rms_scale(stream_in.astype(jnp.float32), attn_gain).astype(jnp.bfloat16)
    projected_rows = jnp.einsum(
        "td,dhc->thc", normed, w_qkv, preferred_element_type=jnp.float32
    ).astype(jnp.bfloat16)
    projected_rows = projected_rows.reshape(
        length_local, heads_local, query_group_width + 2, HEAD_SIZE
    )
    queries = projected_rows[:, :, :query_group_width]
    kv_tail_rows = jnp.concatenate(
        [
            projected_rows[length_local - WINDOW_KEYS :, :, query_group_width],
            projected_rows[length_local - WINDOW_KEYS :, :, query_group_width + 1],
        ],
        axis=-1,
    )
    earlier = from_behind(kv_tail_rows, "seq", 1)
    at_start = lax.axis_index("seq") == 0
    earlier = jnp.where(at_start, key_value_cache, earlier)
    key_rows = jnp.concatenate(
        [earlier[:, :, :HEAD_SIZE], projected_rows[:, :, query_group_width]], axis=0
    )
    value_rows = jnp.concatenate(
        [earlier[:, :, HEAD_SIZE:], projected_rows[:, :, query_group_width + 1]], axis=0
    )
    attended = window_block(queries, key_rows, value_rows).reshape(
        length_local, heads_local * query_group_width * HEAD_SIZE
    )
    block_rows = length_local // tp_count
    attn_out = lax.psum_scatter(
        jnp.dot(attended, w_out, preferred_element_type=jnp.float32).astype(jnp.bfloat16),
        "tp",
        scatter_dimension=0,
        tiled=True,
    ).astype(jnp.float32)
    own_start = lax.axis_index("tp") * block_rows
    residual = (
        lax.dynamic_slice_in_dim(stream_in, own_start, block_rows, 0).astype(jnp.float32) + attn_out
    )
    hidden_in = rms_scale(residual, mlp_gain).astype(jnp.bfloat16)
    experts_dev = w_gateup.shape[0]
    capacity = 2 * length_local * TOPK // (tp_count * EXPERTS)
    blocks = seq_count * tp_count
    group_blocks = max(1, min(blocks, 256 // block_rows))
    groups = blocks // group_blocks
    tokens_all = blocks * block_rows

    index_all = lax.all_gather(expert_index, ("seq", "tp"), axis=0, tiled=True)
    gate_all = lax.all_gather(gate_weight, ("seq", "tp"), axis=0, tiled=True)
    own_experts = lax.axis_index("seq") * experts_dev + jnp.arange(experts_dev, dtype=jnp.int32)
    named = index_all[:, :, None] == own_experts[None, None, :]
    member = jnp.any(named, axis=1).reshape(blocks, block_rows, experts_dev)
    gate_token = jnp.sum(jnp.where(named, gate_all[:, :, None], 0.0), axis=1)
    gate_token = gate_token.reshape(blocks, block_rows, experts_dev)
    rank = jnp.cumsum(member.astype(jnp.int32), axis=1) - 1
    slot = jnp.where(member, rank, -1)
    hot = slot[:, :, :, None] == jnp.arange(capacity, dtype=jnp.int32)
    gate_slot = jnp.sum(hot * gate_token[:, :, :, None], axis=1)
    gate_slot = jnp.moveaxis(gate_slot, 1, 0).reshape(experts_dev, blocks * capacity)
    hot = hot.reshape(groups, group_blocks, block_rows, experts_dev, capacity)
    same = jnp.eye(group_blocks, dtype=jnp.bool_)
    wide = hot[:, :, :, :, None, :] & same[None, :, None, None, :, None]
    placer = wide.reshape(
        groups, group_blocks * block_rows, experts_dev * group_blocks * capacity
    ).astype(jnp.bfloat16)

    tokens = lax.all_gather(hidden_in, ("seq", "tp"), axis=0, tiled=True)
    tokens = tokens.reshape(groups, group_blocks * block_rows, MODEL_WIDTH)
    packed = jnp.einsum("gts,gtd->gsd", placer, tokens, preferred_element_type=jnp.float32)
    packed = packed.astype(jnp.bfloat16).reshape(
        groups, experts_dev, group_blocks * capacity, MODEL_WIDTH
    )

    def one_expert(expert):
        input_rows = packed[:, expert].reshape(-1, MODEL_WIDTH)
        gate_up_rows = jnp.einsum(
            "vi,ipk->vpk", input_rows, w_gateup[expert], preferred_element_type=jnp.float32
        )
        activated = jax.nn.silu(gate_up_rows[:, 0]) * gate_up_rows[:, 1]
        activated = (activated * gate_slot[expert][:, None]).astype(jnp.bfloat16)
        result = jnp.dot(activated, w_down[expert], preferred_element_type=jnp.float32)
        return result.astype(jnp.bfloat16).reshape(groups, group_blocks * capacity, MODEL_WIDTH)

    results = jnp.stack([one_expert(expert) for expert in range(experts_dev)], axis=1)
    results = results.reshape(groups, experts_dev * group_blocks * capacity, MODEL_WIDTH)
    summed = jnp.einsum("gts,gsd->gtd", placer, results, preferred_element_type=jnp.float32)
    summed = summed.astype(jnp.bfloat16).reshape(tokens_all, MODEL_WIDTH)
    mixture = lax.psum_scatter(summed, ("seq", "tp"), scatter_dimension=0, tiled=True)
    return (residual + mixture.astype(jnp.float32)).astype(jnp.bfloat16)


def solution(mesh):
    in_specs = (
        P("seq", None),
        P(),
        P(None, "tp", None),
        P(None, "tp", None),
        P("tp", None),
        P(),
        P(("seq", "tp"), None),
        P(("seq", "tp"), None),
        P("seq", None, None, "tp"),
        P("seq", "tp", None),
    )
    out_specs = P(("seq", "tp"), None)
    return jax.shard_map(local, mesh=mesh, in_specs=in_specs, out_specs=out_specs, check_vma=False)
```

```python
import jax
import jax.numpy as jnp
from jax import lax
from jax.sharding import PartitionSpec as P

MODEL_WIDTH = 2880
QUERY_HEADS = 64
KEY_VALUE_HEADS = 8
HEAD_SIZE = 64
WINDOW_KEYS = 128
EXPERTS = 32
TOPK = 4


EPS = 1e-05


def from_behind(value, axis, steps):
    count = lax.axis_size(axis)
    first, last = (max(0, -steps), min(count, count - steps))
    return lax.ppermute(value, axis, [(source, source + steps) for source in range(first, last)])


def axis_plan(seq_count, tp_count):
    across = tp_count // 2
    slow = min(4, seq_count)
    quick = seq_count // slow
    x_step, quick_step, slow_step = 2, 2 * across, 2 * across * quick
    along = [(slow, slow_step, slow_step)]
    if across == quick:
        along.append((across, x_step, quick_step))
        along.append((across, quick_step, x_step))
    else:
        along.append((across, x_step, x_step))
        along.append((quick, quick_step, quick_step))
    return [step for step in along if step[0] > 1]


def swap(value, even_mask, odd_mask):
    count = lax.axis_size("seq") * lax.axis_size("tp")
    pairs = [
        (device, device ^ (odd_mask if device % 2 else even_mask)) for device in range(count)
    ]
    return lax.ppermute(value, ("seq", "tp"), pairs)


def spread(rows, plan):
    held = rows
    for size, even, odd in plan:
        others = [swap(held, other * even, other * odd) for other in range(1, size)]
        held = jnp.concatenate([held] + others, axis=0)
    return held


def collect(sums, plan):
    held = sums
    for size, even, odd in reversed(plan):
        parts = held.reshape(size, held.shape[0] // size, held.shape[1])
        total = parts[0].astype(jnp.float32)
        for other in range(1, size):
            arrived = swap(parts[other].astype(jnp.bfloat16), other * even, other * odd)
            total = total + arrived.astype(jnp.float32)
        held = total
    return held


def rms_scale(values, gain_vec):
    mean_sq = jnp.mean(values * values, axis=-1, keepdims=True)
    return values * lax.rsqrt(mean_sq + EPS) * gain_vec


def window_block(queries, key_rows, value_rows):
    scores = jnp.einsum(
        "qhgc,khc->hgqk", queries, key_rows, preferred_element_type=jnp.float32
    ) * HEAD_SIZE ** (-0.5)
    key_offset = jnp.arange(key_rows.shape[0])[None, :] - jnp.arange(queries.shape[0])[:, None]
    in_window = (key_offset >= 1) & (key_offset <= WINDOW_KEYS)
    scores = jnp.where(in_window, scores, -1e30)
    row_max = jnp.max(scores, axis=-1, keepdims=True)
    exponent = jnp.exp(scores - row_max)
    layer_weights = (exponent / jnp.sum(exponent, axis=-1, keepdims=True)).astype(jnp.bfloat16)
    attended = jnp.einsum(
        "hgqk,khc->qhgc", layer_weights, value_rows, preferred_element_type=jnp.float32
    )
    return attended.astype(jnp.bfloat16)


def local(
    stream_in,
    attn_gain,
    w_qkv,
    key_value_cache,
    w_out,
    mlp_gain,
    expert_index,
    gate_weight,
    w_gateup,
    w_down,
):
    seq_count = lax.axis_size("seq")
    tp_count = lax.axis_size("tp")
    length_local = stream_in.shape[0]
    heads_local = w_qkv.shape[1]
    query_group_width = QUERY_HEADS // KEY_VALUE_HEADS
    normed = rms_scale(stream_in.astype(jnp.float32), attn_gain).astype(jnp.bfloat16)
    projected_rows = jnp.einsum(
        "td,dhc->thc", normed, w_qkv, preferred_element_type=jnp.float32
    ).astype(jnp.bfloat16)
    projected_rows = projected_rows.reshape(
        length_local, heads_local, query_group_width + 2, HEAD_SIZE
    )
    queries = projected_rows[:, :, :query_group_width]
    kv_tail_rows = jnp.concatenate(
        [
            projected_rows[length_local - WINDOW_KEYS :, :, query_group_width],
            projected_rows[length_local - WINDOW_KEYS :, :, query_group_width + 1],
        ],
        axis=-1,
    )
    earlier = from_behind(kv_tail_rows, "seq", 1)
    at_start = lax.axis_index("seq") == 0
    earlier = jnp.where(at_start, key_value_cache, earlier)
    key_rows = jnp.concatenate(
        [earlier[:, :, :HEAD_SIZE], projected_rows[:, :, query_group_width]], axis=0
    )
    value_rows = jnp.concatenate(
        [earlier[:, :, HEAD_SIZE:], projected_rows[:, :, query_group_width + 1]], axis=0
    )
    attended = window_block(queries, key_rows, value_rows).reshape(
        length_local, heads_local * query_group_width * HEAD_SIZE
    )
    block_rows = length_local // tp_count
    plan = axis_plan(seq_count, tp_count)
    across = tp_count // 2

    terms = jnp.dot(attended, w_out, preferred_element_type=jnp.float32)
    terms = terms.reshape(across, 2, block_rows, MODEL_WIDTH)
    core = lax.axis_index("tp") % 2
    kept = lax.dynamic_index_in_dim(terms, core, 1, False)
    handed = lax.dynamic_index_in_dim(terms, 1 - core, 1, False).astype(jnp.bfloat16)
    kept = kept + swap(handed, 1, 1).astype(jnp.float32)
    place = lax.axis_index("tp") // 2
    attn_out = lax.dynamic_index_in_dim(kept, place, 0, False)
    for other in range(1, across):
        part = lax.dynamic_index_in_dim(kept, place ^ other, 0, False).astype(jnp.bfloat16)
        attn_out = attn_out + swap(part, 2 * other, 2 * other).astype(jnp.float32)
    own_start = lax.axis_index("tp") * block_rows
    residual = (
        lax.dynamic_slice_in_dim(stream_in, own_start, block_rows, 0).astype(jnp.float32) + attn_out
    )
    hidden_in = rms_scale(residual, mlp_gain).astype(jnp.bfloat16)

    experts_dev = w_gateup.shape[0]
    capacity = 2 * length_local * TOPK // (tp_count * EXPERTS)
    blocks = seq_count * tp_count
    group_blocks = max(1, min(blocks // 2, 256 // block_rows))
    groups = blocks // group_blocks

    high = lax.reduce_precision(gate_weight, 8, 7)
    middle = lax.reduce_precision(gate_weight - high, 8, 7)
    low = lax.reduce_precision(gate_weight - high - middle, 8, 7)
    routing = jnp.concatenate([expert_index.astype(jnp.float32), high, middle, low], axis=1)
    routing = jnp.pad(routing, ((0, 0), (0, 64 - 4 * TOPK))).astype(jnp.bfloat16)
    rows = jnp.concatenate([hidden_in, routing], axis=1)

    mine = spread(rows, plan)
    theirs = swap(mine, 1, 1)
    tokens = jnp.concatenate([mine, theirs], axis=0)

    routing = tokens[:, MODEL_WIDTH:].astype(jnp.float32)
    index_all = routing[:, :TOPK].astype(jnp.int32)
    gate_all = (
        routing[:, TOPK : 2 * TOPK]
        + routing[:, 2 * TOPK : 3 * TOPK]
        + routing[:, 3 * TOPK : 4 * TOPK]
    )
    own_experts = lax.axis_index("seq") * experts_dev + jnp.arange(experts_dev, dtype=jnp.int32)
    named = index_all[:, :, None] == own_experts[None, None, :]
    member = jnp.any(named, axis=1).reshape(blocks, block_rows, experts_dev)
    gate_token = jnp.sum(jnp.where(named, gate_all[:, :, None], 0.0), axis=1)
    gate_token = gate_token.reshape(blocks, block_rows, experts_dev)
    rank = jnp.cumsum(member.astype(jnp.int32), axis=1) - 1
    slot = jnp.where(member, rank, -1)
    hot = slot[:, :, :, None] == jnp.arange(capacity, dtype=jnp.int32)
    gate_slot = jnp.sum(hot * gate_token[:, :, :, None], axis=1)
    gate_slot = jnp.moveaxis(gate_slot, 1, 0).reshape(experts_dev, blocks * capacity)
    hot = hot.reshape(groups, group_blocks, block_rows, experts_dev, capacity)
    same = jnp.eye(group_blocks, dtype=jnp.bool_)
    wide = hot[:, :, :, :, None, :] & same[None, :, None, None, :, None]
    placer = wide.reshape(
        groups, group_blocks * block_rows, experts_dev * group_blocks * capacity
    ).astype(jnp.bfloat16)

    tokens = tokens[:, :MODEL_WIDTH].reshape(groups, group_blocks * block_rows, MODEL_WIDTH)
    packed = jnp.einsum("gts,gtd->gsd", placer, tokens, preferred_element_type=jnp.float32)
    packed = packed.astype(jnp.bfloat16).reshape(
        groups, experts_dev, group_blocks * capacity, MODEL_WIDTH
    )

    def one_expert(expert):
        input_rows = packed[:, expert].reshape(-1, MODEL_WIDTH)
        gate_up_rows = jnp.einsum(
            "vi,ipk->vpk", input_rows, w_gateup[expert], preferred_element_type=jnp.float32
        )
        activated = jax.nn.silu(gate_up_rows[:, 0]) * gate_up_rows[:, 1]
        activated = (activated * gate_slot[expert][:, None]).astype(jnp.bfloat16)
        result = jnp.dot(activated, w_down[expert], preferred_element_type=jnp.float32)
        return result.astype(jnp.bfloat16).reshape(groups, group_blocks * capacity, MODEL_WIDTH)

    results = jnp.stack([one_expert(expert) for expert in range(experts_dev)], axis=1)
    results = results.reshape(groups, experts_dev * group_blocks * capacity, MODEL_WIDTH)
    summed = jnp.einsum("gts,gsd->gtd", placer, results, preferred_element_type=jnp.float32)
    summed = summed.astype(jnp.bfloat16).reshape(2, blocks // 2 * block_rows, MODEL_WIDTH)
    kept_sums = summed[0].astype(jnp.float32) + swap(summed[1], 1, 1).astype(jnp.float32)
    mixture = collect(kept_sums, plan)
    return (residual + mixture).astype(jnp.bfloat16)


def solution(mesh):
    in_specs = (
        P("seq", None),
        P(),
        P(None, "tp", None),
        P(None, "tp", None),
        P("tp", None),
        P(),
        P(("seq", "tp"), None),
        P(("seq", "tp"), None),
        P("seq", None, None, "tp"),
        P("seq", "tp", None),
    )
    out_specs = P(("seq", "tp"), None)
    return jax.shard_map(local, mesh=mesh, in_specs=in_specs, out_specs=out_specs, check_vma=False)
```

```python
import functools

import jax
import jax.numpy as jnp
from jax import lax
from jax.experimental import pallas as pl
from jax.experimental.pallas import tpu as pltpu
from jax.sharding import PartitionSpec as P

MODEL_WIDTH = 2880
QUERY_HEADS = 64
KEY_VALUE_HEADS = 8
HEAD_SIZE = 64
WINDOW_KEYS = 128
EXPERTS = 32
TOPK = 4


EPS = 1e-05


def from_behind(value, axis, steps):
    count = lax.axis_size(axis)
    first, last = (max(0, -steps), min(count, count - steps))
    return lax.ppermute(value, axis, [(source, source + steps) for source in range(first, last)])


def axis_plan(seq_count, tp_count):
    across = tp_count // 2
    slow = min(4, seq_count)
    quick = seq_count // slow
    x_step, quick_step, slow_step = 2, 2 * across, 2 * across * quick
    along = [(slow, slow_step, slow_step)]
    if across == quick:
        along.append((across, x_step, quick_step))
        along.append((across, quick_step, x_step))
    else:
        along.append((across, x_step, x_step))
        along.append((quick, quick_step, quick_step))
    return along


def swap(value, even_mask, odd_mask):
    count = lax.axis_size("seq") * lax.axis_size("tp")
    pairs = [
        (device, device ^ (odd_mask if device % 2 else even_mask)) for device in range(count)
    ]
    return lax.ppermute(value, ("seq", "tp"), pairs)


def spread(piece, steps):
    pieces = [piece]
    for size, even, odd in steps:
        pieces = pieces + [
            swap(held, other * even, other * odd) for other in range(1, size) for held in pieces
        ]
    return pieces


def collect(sums, steps):
    held = sums
    for size, even, odd in reversed(steps):
        parts = held.reshape(size, held.shape[0] // size, held.shape[1])
        total = parts[0].astype(jnp.float32)
        for other in range(1, size):
            arrived = swap(parts[other].astype(jnp.bfloat16), other * even, other * odd)
            total = total + arrived.astype(jnp.float32)
        held = total
    return held


ROUTING = 64


def gate_up_kernel(sizes, first_ref, *refs):
    groups, per_group, block_rows, capacity, experts = sizes
    pieces = refs[: groups * per_group]
    weight_ref, act_ref, placer_ref, packed_ref, gate_ref = refs[groups * per_group :]
    tokens_n = per_group * block_rows
    span = per_group * capacity
    slots_n = experts * span

    @pl.when((pl.program_id(0) == 0) & (pl.program_id(1) == 0))
    def _():
        slot = lax.broadcasted_iota(jnp.int32, (slots_n, tokens_n), 0)
        token = lax.broadcasted_iota(jnp.int32, (slots_n, tokens_n), 1)
        expert_of = (slot // span + first_ref[0]).astype(jnp.float32)
        place_of = (slot % capacity).astype(jnp.float32)
        own_block = (slot // capacity) % per_group == token // block_rows
        before = lax.broadcasted_iota(jnp.int32, (tokens_n, tokens_n), 0)
        after = lax.broadcasted_iota(jnp.int32, (tokens_n, tokens_n), 1)
        earlier = (before // block_rows == after // block_rows) & (before < after)
        earlier = jnp.where(earlier, 1.0, 0.0).astype(jnp.bfloat16)
        for group in range(groups):
            held = pieces[group * per_group : (group + 1) * per_group]
            rows = jnp.concatenate([piece[:, :MODEL_WIDTH] for piece in held], axis=0)
            start = MODEL_WIDTH + ROUTING - 128
            tail = jnp.concatenate([piece[:, start : start + 128] for piece in held], axis=0)
            tail = jnp.transpose(tail.astype(jnp.float32))[128 - ROUTING :]
            member = jnp.zeros((slots_n, tokens_n), jnp.float32)
            gate = jnp.zeros((slots_n, tokens_n), jnp.float32)
            for choice in range(TOPK):
                hit = tail[choice : choice + 1] == expert_of
                weight = (
                    tail[TOPK + choice : TOPK + choice + 1]
                    + tail[2 * TOPK + choice : 2 * TOPK + choice + 1]
                    + tail[3 * TOPK + choice : 3 * TOPK + choice + 1]
                )
                member = member + jnp.where(hit, 1.0, 0.0)
                gate = gate + jnp.where(hit, weight, 0.0)
            rank = jnp.dot(
                member.astype(jnp.bfloat16), earlier, preferred_element_type=jnp.float32
            )
            chosen = own_block & (rank == place_of) & (member > 0.5)
            hot = jnp.where(chosen, 1.0, 0.0)
            gate = jnp.sum(jnp.where(chosen, gate, 0.0), axis=1, keepdims=True)
            placer_ref[group] = jnp.transpose(hot).astype(jnp.bfloat16)
            packed = jnp.dot(hot.astype(jnp.bfloat16), rows, preferred_element_type=jnp.float32)
            packed = packed.astype(jnp.bfloat16)
            for expert in range(experts):
                place = slice(group * span, (group + 1) * span)
                packed_ref[expert, place] = packed[expert * span : (expert + 1) * span]
                gate_ref[expert, place] = jnp.broadcast_to(
                    gate[expert * span : (expert + 1) * span], (span, 128)
                )

    expert = pl.program_id(0)
    units = weight_ref.shape[2]
    rows = packed_ref[expert]
    contract = (((1,), (1,)), ((), ()))
    gate = lax.dot_general(weight_ref[0, 0], rows, contract, preferred_element_type=jnp.float32)
    up = lax.dot_general(weight_ref[0, 1], rows, contract, preferred_element_type=jnp.float32)
    scale = jnp.transpose(gate_ref[expert])[0:1]
    act_ref[0] = (gate / (1.0 + jnp.exp(-gate)) * up * scale).astype(jnp.bfloat16)


def gate_up(first, pieces, weights, block_rows, capacity):
    groups, per_group = len(pieces), len(pieces[0])
    experts, _, units, width = weights.shape
    slots = groups * per_group * capacity
    tokens_n = per_group * block_rows
    unit_block = 240 if units % 240 == 0 else units
    flat = [piece for group in pieces for piece in group]
    sizes = (groups, per_group, block_rows, capacity, experts)
    whole = pl.BlockSpec(
        (block_rows, width + ROUTING), lambda e, f: (0, 0), pipeline_mode=pl.Buffered(1)
    )
    return pl.pallas_call(
        functools.partial(gate_up_kernel, sizes),
        grid=(experts, units // unit_block),
        in_specs=[pl.BlockSpec(memory_space=pltpu.SMEM)]
        + [whole] * len(flat)
        + [
            pl.BlockSpec((1, 2, unit_block, width), lambda e, f: (e, 0, f, 0)),
        ],
        out_specs=[
            pl.BlockSpec((1, unit_block, slots), lambda e, f: (e, f, 0)),
            pl.BlockSpec((groups, tokens_n, experts * per_group * capacity), lambda e, f: (0, 0, 0)),
        ],
        out_shape=[
            jax.ShapeDtypeStruct((experts, units, slots), jnp.bfloat16),
            jax.ShapeDtypeStruct(
                (groups, tokens_n, experts * per_group * capacity), jnp.bfloat16
            ),
        ],
        scratch_shapes=[
            pltpu.VMEM((experts, slots, width), jnp.bfloat16),
            pltpu.VMEM((experts, slots, 128), jnp.float32),
        ],
        compiler_params=pltpu.CompilerParams(vmem_limit_bytes=48 << 20),
        cost_estimate=pl.CostEstimate(
            flops=4 * experts * slots * width * units,
            bytes_accessed=4 * experts * width * units,
            transcendentals=0,
        ),
    )(first, *flat, weights)


def down_kernel(groups, act_ref, weight_ref, out_ref):
    rows = jnp.transpose(act_ref[0].astype(jnp.float32)).astype(jnp.bfloat16)
    result = jnp.dot(rows, weight_ref[0], preferred_element_type=jnp.float32)
    out_ref[...] = result.astype(jnp.bfloat16).reshape(out_ref.shape)


def down(act, weights, groups):
    experts, units, slots = act.shape
    width = weights.shape[2]
    span = slots // groups
    return pl.pallas_call(
        functools.partial(down_kernel, groups),
        grid=(experts,),
        in_specs=[
            pl.BlockSpec((1, units, slots), lambda e: (e, 0, 0)),
            pl.BlockSpec((1, units, width), lambda e: (e, 0, 0)),
        ],
        out_specs=pl.BlockSpec((groups, span, width), lambda e: (0, e, 0)),
        out_shape=jax.ShapeDtypeStruct((groups, experts * span, width), jnp.bfloat16),
        compiler_params=pltpu.CompilerParams(vmem_limit_bytes=48 << 20),
        cost_estimate=pl.CostEstimate(
            flops=2 * experts * slots * width * units,
            bytes_accessed=2 * experts * width * units,
            transcendentals=0,
        ),
    )(act, weights)


def unpack_kernel(placer_ref, result_ref, mine_ref, theirs_ref):
    summed = jnp.dot(placer_ref[0], result_ref[0], preferred_element_type=jnp.float32)
    summed = summed.astype(jnp.bfloat16)
    half = mine_ref.shape[0]
    mine_ref[...] = summed[:half]
    theirs_ref[...] = summed[half:]


def unpack(placer, results, group):
    _, tokens_n, slots = placer.shape
    width = results.shape[2]
    half = jax.ShapeDtypeStruct((tokens_n // 2, width), jnp.bfloat16)
    return pl.pallas_call(
        unpack_kernel,
        grid=(1,),
        in_specs=[
            pl.BlockSpec((1, tokens_n, slots), lambda i: (group, 0, 0)),
            pl.BlockSpec((1, slots, width), lambda i: (group, 0, 0)),
        ],
        out_specs=[pl.BlockSpec(half.shape, lambda i: (0, 0))] * 2,
        out_shape=[half, half],
        compiler_params=pltpu.CompilerParams(vmem_limit_bytes=32 << 20),
        cost_estimate=pl.CostEstimate(
            flops=2 * tokens_n * slots * width,
            bytes_accessed=2 * (tokens_n + slots) * width,
            transcendentals=0,
        ),
    )(placer, results)


def rms_scale(values, gain_vec):
    mean_sq = jnp.mean(values * values, axis=-1, keepdims=True)
    return values * lax.rsqrt(mean_sq + EPS) * gain_vec


def window_block(queries, key_rows, value_rows):
    scores = jnp.einsum(
        "qhgc,khc->hgqk", queries, key_rows, preferred_element_type=jnp.float32
    ) * HEAD_SIZE ** (-0.5)
    key_offset = jnp.arange(key_rows.shape[0])[None, :] - jnp.arange(queries.shape[0])[:, None]
    in_window = (key_offset >= 1) & (key_offset <= WINDOW_KEYS)
    scores = jnp.where(in_window, scores, -1e30)
    row_max = jnp.max(scores, axis=-1, keepdims=True)
    exponent = jnp.exp(scores - row_max)
    layer_weights = (exponent / jnp.sum(exponent, axis=-1, keepdims=True)).astype(jnp.bfloat16)
    attended = jnp.einsum(
        "hgqk,khc->qhgc", layer_weights, value_rows, preferred_element_type=jnp.float32
    )
    return attended.astype(jnp.bfloat16)


def local(
    stream_in,
    attn_gain,
    w_qkv,
    key_value_cache,
    w_out,
    mlp_gain,
    expert_index,
    gate_weight,
    w_gateup,
    w_down,
):
    seq_count = lax.axis_size("seq")
    tp_count = lax.axis_size("tp")
    length_local = stream_in.shape[0]
    heads_local = w_qkv.shape[1]
    query_group_width = QUERY_HEADS // KEY_VALUE_HEADS
    normed = rms_scale(stream_in.astype(jnp.float32), attn_gain).astype(jnp.bfloat16)
    projected_rows = jnp.einsum(
        "td,dhc->thc", normed, w_qkv, preferred_element_type=jnp.float32
    ).astype(jnp.bfloat16)
    projected_rows = projected_rows.reshape(
        length_local, heads_local, query_group_width + 2, HEAD_SIZE
    )
    queries = projected_rows[:, :, :query_group_width]
    kv_tail_rows = jnp.concatenate(
        [
            projected_rows[length_local - WINDOW_KEYS :, :, query_group_width],
            projected_rows[length_local - WINDOW_KEYS :, :, query_group_width + 1],
        ],
        axis=-1,
    )
    earlier = from_behind(kv_tail_rows, "seq", 1)
    at_start = lax.axis_index("seq") == 0
    earlier = jnp.where(at_start, key_value_cache, earlier)
    key_rows = jnp.concatenate(
        [earlier[:, :, :HEAD_SIZE], projected_rows[:, :, query_group_width]], axis=0
    )
    value_rows = jnp.concatenate(
        [earlier[:, :, HEAD_SIZE:], projected_rows[:, :, query_group_width + 1]], axis=0
    )
    attended = window_block(queries, key_rows, value_rows).reshape(
        length_local, heads_local * query_group_width * HEAD_SIZE
    )
    block_rows = length_local // tp_count
    plan = axis_plan(seq_count, tp_count)
    across = tp_count // 2

    terms = jnp.dot(attended, w_out, preferred_element_type=jnp.float32)
    terms = terms.reshape(across, 2, block_rows, MODEL_WIDTH)
    core = lax.axis_index("tp") % 2
    kept = lax.dynamic_index_in_dim(terms, core, 1, False)
    handed = lax.dynamic_index_in_dim(terms, 1 - core, 1, False).astype(jnp.bfloat16)
    kept = kept + swap(handed, 1, 1).astype(jnp.float32)
    place = lax.axis_index("tp") // 2
    attn_out = lax.dynamic_index_in_dim(kept, place, 0, False)
    for other in range(1, across):
        part = lax.dynamic_index_in_dim(kept, place ^ other, 0, False).astype(jnp.bfloat16)
        attn_out = attn_out + swap(part, 2 * other, 2 * other).astype(jnp.float32)
    own_start = lax.axis_index("tp") * block_rows
    residual = (
        lax.dynamic_slice_in_dim(stream_in, own_start, block_rows, 0).astype(jnp.float32) + attn_out
    )
    hidden_in = rms_scale(residual, mlp_gain).astype(jnp.bfloat16)

    experts_dev = w_gateup.shape[0]
    capacity = 2 * length_local * TOPK // (tp_count * EXPERTS)
    high = lax.reduce_precision(gate_weight, 8, 7)
    middle = lax.reduce_precision(gate_weight - high, 8, 7)
    low = lax.reduce_precision(gate_weight - high - middle, 8, 7)
    routing = jnp.concatenate([expert_index.astype(jnp.float32), high, middle, low], axis=1)
    routing = jnp.pad(routing, ((0, 0), (0, ROUTING - 4 * TOPK))).astype(jnp.bfloat16)
    rows = jnp.concatenate([hidden_in, routing], axis=1)

    (slow, slow_step, _), inner = plan[0], plan[1:]
    held = [rows] + [swap(rows, other * slow_step, other * slow_step) for other in range(1, slow)]
    mine = [spread(piece, inner) for piece in held]
    pieces = [group + [swap(piece, 1, 1) for piece in group] for group in mine]

    first = (lax.axis_index("seq") * experts_dev).astype(jnp.int32).reshape(1)
    weights = jnp.transpose(w_gateup, (0, 2, 3, 1))
    act, placer = gate_up(first, pieces, weights, block_rows, capacity)
    results = down(act, w_down, slow)

    total = residual
    for group in list(range(1, slow)) + [0]:
        kept, handed = unpack(placer, results, group)
        sums = kept.astype(jnp.float32) + swap(handed, 1, 1).astype(jnp.float32)
        sums = collect(sums, inner)
        if group:
            sums = swap(sums.astype(jnp.bfloat16), group * slow_step, group * slow_step)
        total = total + sums.astype(jnp.float32)
    return total.astype(jnp.bfloat16)


def solution(mesh):
    in_specs = (
        P("seq", None),
        P(),
        P(None, "tp", None),
        P(None, "tp", None),
        P("tp", None),
        P(),
        P(("seq", "tp"), None),
        P(("seq", "tp"), None),
        P("seq", None, None, "tp"),
        P("seq", "tp", None),
    )
    out_specs = P(("seq", "tp"), None)
    return jax.shard_map(local, mesh=mesh, in_specs=in_specs, out_specs=out_specs, check_vma=False)
```

```python
import functools

import jax
import jax.numpy as jnp
from jax import lax
from jax.experimental import pallas as pl
from jax.experimental.pallas import tpu as pltpu
from jax.sharding import PartitionSpec as P

MODEL_WIDTH = 2880
QUERY_HEADS = 64
KEY_VALUE_HEADS = 8
HEAD_SIZE = 64
WINDOW_KEYS = 128
EXPERTS = 32
TOPK = 4


EPS = 1e-05


def from_behind(value, axis, steps):
    count = lax.axis_size(axis)
    first, last = (max(0, -steps), min(count, count - steps))
    return lax.ppermute(value, axis, [(source, source + steps) for source in range(first, last)])


def axis_plan(seq_count, tp_count):
    across = tp_count // 2
    slow = min(4, seq_count)
    quick = seq_count // slow
    x_step, quick_step, slow_step = 2, 2 * across, 2 * across * quick
    along = [(slow, slow_step, slow_step)]
    if across == quick:
        along.append((across, x_step, quick_step))
        along.append((across, quick_step, x_step))
    else:
        along.append((across, x_step, x_step))
        along.append((quick, quick_step, quick_step))
    return along


def swap(value, even_mask, odd_mask):
    count = lax.axis_size("seq") * lax.axis_size("tp")
    pairs = [
        (device, device ^ (odd_mask if device % 2 else even_mask)) for device in range(count)
    ]
    return lax.ppermute(value, ("seq", "tp"), pairs)


def spread(piece, steps):
    pieces = [piece]
    for size, even, odd in steps:
        pieces = pieces + [
            swap(held, other * even, other * odd) for other in range(1, size) for held in pieces
        ]
    return pieces


ROUTING = 64


def join_kernel(*refs):
    parts, out_ref = refs[:-1], refs[-1]
    rows = parts[0].shape[0]
    for place, part in enumerate(parts):
        out_ref[place * rows : (place + 1) * rows, :] = part[...]


def join(parts):
    rows, width = parts[0].shape
    return pl.pallas_call(
        join_kernel,
        out_shape=jax.ShapeDtypeStruct((len(parts) * rows, width), parts[0].dtype),
        cost_estimate=pl.CostEstimate(
            flops=0, bytes_accessed=4 * len(parts) * rows * width, transcendentals=0
        ),
    )(*parts)


def fold_kernel(count, *refs):
    terms, outs = refs[:count], refs[count:]
    rows = outs[0].shape[0]
    for place, out_ref in enumerate(outs):
        cut = slice(place * rows, (place + 1) * rows)
        total = terms[0][cut, :].astype(jnp.float32)
        for term in terms[1:]:
            total = total + term[cut, :].astype(jnp.float32)
        out_ref[...] = total.astype(out_ref.dtype)


def fold(terms, parts):
    rows, width = terms[0].shape
    rows = rows // parts
    kinds = [jnp.float32] + [jnp.bfloat16] * (parts - 1)
    return pl.pallas_call(
        functools.partial(fold_kernel, len(terms)),
        out_shape=[jax.ShapeDtypeStruct((rows, width), kind) for kind in kinds],
        cost_estimate=pl.CostEstimate(
            flops=len(terms) * rows * parts * width,
            bytes_accessed=4 * len(terms) * rows * parts * width,
            transcendentals=0,
        ),
    )(*terms)


def collect(kept, arrived, steps):
    terms = [kept, arrived]
    for size, even, odd in reversed(steps):
        parts = fold(terms, size)
        terms = [parts[0]] + [
            swap(parts[other], other * even, other * odd) for other in range(1, size)
        ]
    return fold(terms, 1)[0]


def expert_kernel(sizes, first_ref, *refs):
    groups, per_group, block_rows, capacity = sizes
    halves = refs[: 2 * groups]
    gate_up_ref, down_ref = refs[2 * groups : 2 * groups + 2]
    outs = refs[2 * groups + 2 : 4 * groups + 2]
    tokens_ref, gate_up_buf, down_buf, packed_ref, gate_ref, placer_ref = refs[4 * groups + 2 : -4]
    token_sem, gate_up_sem, down_sem, out_sem = refs[-4:]
    experts, _, units, width = gate_up_ref.shape
    tokens_n = per_group * block_rows
    half = tokens_n // 2
    span = per_group * capacity
    slots_n = experts * span

    def token_copy(group, side):
        return pltpu.make_async_copy(
            halves[2 * group + side],
            tokens_ref.at[group, pl.ds(side * half, half)],
            token_sem.at[group, side],
        )

    def out_copy(group, side):
        return pltpu.make_async_copy(
            tokens_ref.at[group, pl.ds(side * half, half)],
            outs[2 * group + side],
            out_sem.at[group, side],
        )

    def gate_up_copy(expert):
        return pltpu.make_async_copy(
            gate_up_ref.at[expert], gate_up_buf.at[expert % 2], gate_up_sem.at[expert % 2]
        )

    def down_copy(expert):
        return pltpu.make_async_copy(
            down_ref.at[expert], down_buf.at[expert % 2], down_sem.at[expert % 2]
        )

    for group in range(groups):
        for side in range(2):
            token_copy(group, side).start()
    gate_up_copy(0).start()
    down_copy(0).start()

    slot = lax.broadcasted_iota(jnp.int32, (slots_n, tokens_n), 0)
    token = lax.broadcasted_iota(jnp.int32, (slots_n, tokens_n), 1)
    expert_of = (slot // span + first_ref[0]).astype(jnp.float32)
    place_of = (slot % capacity).astype(jnp.float32)
    own_block = (slot // capacity) % per_group == token // block_rows
    before = lax.broadcasted_iota(jnp.int32, (tokens_n, tokens_n), 0)
    after = lax.broadcasted_iota(jnp.int32, (tokens_n, tokens_n), 1)
    earlier = (before // block_rows == after // block_rows) & (before < after)
    earlier = jnp.where(earlier, 1.0, 0.0).astype(jnp.bfloat16)
    start = width + ROUTING - 128
    for group in range(groups):
        for side in range(2):
            token_copy(group, side).wait()
        tail = tokens_ref[group, :, start : start + 128].astype(jnp.float32)
        tail = jnp.transpose(tail)[128 - ROUTING :]
        member = jnp.zeros((slots_n, tokens_n), jnp.float32)
        gate = jnp.zeros((slots_n, tokens_n), jnp.float32)
        for choice in range(TOPK):
            hit = tail[choice : choice + 1] == expert_of
            weight = (
                tail[TOPK + choice : TOPK + choice + 1]
                + tail[2 * TOPK + choice : 2 * TOPK + choice + 1]
                + tail[3 * TOPK + choice : 3 * TOPK + choice + 1]
            )
            member = member + jnp.where(hit, 1.0, 0.0)
            gate = gate + jnp.where(hit, weight, 0.0)
        rank = jnp.dot(member.astype(jnp.bfloat16), earlier, preferred_element_type=jnp.float32)
        chosen = own_block & (rank == place_of) & (member > 0.5)
        hot = jnp.where(chosen, 1.0, 0.0)
        gate = jnp.sum(jnp.where(chosen, gate, 0.0), axis=1, keepdims=True)
        placer_ref[group] = jnp.transpose(hot).astype(jnp.bfloat16)
        rows = tokens_ref[group, :, :width]
        packed = jnp.dot(hot.astype(jnp.bfloat16), rows, preferred_element_type=jnp.float32)
        packed = packed.astype(jnp.bfloat16)
        for expert in range(experts):
            place = slice(group * span, (group + 1) * span)
            packed_ref[expert, place] = packed[expert * span : (expert + 1) * span]
            gate_ref[expert, place] = jnp.broadcast_to(
                gate[expert * span : (expert + 1) * span], (span, 128)
            )

    for expert in range(experts):
        if expert + 1 < experts:
            gate_up_copy(expert + 1).start()
            down_copy(expert + 1).start()
        gate_up_copy(expert).wait()
        both = lax.dot_general(
            gate_up_buf[expert % 2].reshape(2 * units, width),
            packed_ref[expert],
            (((1,), (1,)), ((), ())),
            preferred_element_type=jnp.float32,
        )
        gate, up = both[:units], both[units:]
        scale = jnp.transpose(gate_ref[expert])[0:1]
        act = gate / (1.0 + jnp.exp(-gate)) * up * scale
        act = jnp.transpose(act).astype(jnp.bfloat16)
        down_copy(expert).wait()
        result = jnp.dot(act, down_buf[expert % 2], preferred_element_type=jnp.float32)
        packed_ref[expert] = result.astype(jnp.bfloat16)

    for group in range(groups):
        place = slice(group * span, (group + 1) * span)
        rows = jnp.concatenate([packed_ref[expert, place] for expert in range(experts)], axis=0)
        summed = jnp.dot(placer_ref[group], rows, preferred_element_type=jnp.float32)
        tokens_ref[group, :, :width] = summed.astype(jnp.bfloat16)
        for side in range(2):
            out_copy(group, side).start()
    for group in range(groups):
        for side in range(2):
            out_copy(group, side).wait()


def run_experts(first, halves, gate_up, down, block_rows, capacity):
    groups = len(halves) // 2
    half, wide = halves[0].shape
    experts, _, units, width = gate_up.shape
    per_group = 2 * half // block_rows
    slots_n = experts * per_group * capacity
    anywhere = pl.BlockSpec(memory_space=pl.ANY)
    out = jax.ShapeDtypeStruct((half, wide), jnp.bfloat16)
    return pl.pallas_call(
        functools.partial(expert_kernel, (groups, per_group, block_rows, capacity)),
        in_specs=[pl.BlockSpec(memory_space=pltpu.SMEM)] + [anywhere] * (2 * groups + 2),
        out_specs=[anywhere] * (2 * groups),
        out_shape=[out] * (2 * groups),
        scratch_shapes=[
            pltpu.VMEM((groups, 2 * half, wide), jnp.bfloat16),
            pltpu.VMEM((2, 2, units, width), jnp.bfloat16),
            pltpu.VMEM((2, units, width), jnp.bfloat16),
            pltpu.VMEM((experts, groups * per_group * capacity, width), jnp.bfloat16),
            pltpu.VMEM((experts, groups * per_group * capacity, 128), jnp.float32),
            pltpu.VMEM((groups, 2 * half, slots_n), jnp.bfloat16),
            pltpu.SemaphoreType.DMA((groups, 2)),
            pltpu.SemaphoreType.DMA((2,)),
            pltpu.SemaphoreType.DMA((2,)),
            pltpu.SemaphoreType.DMA((groups, 2)),
        ],
        compiler_params=pltpu.CompilerParams(vmem_limit_bytes=54 << 20),
        cost_estimate=pl.CostEstimate(
            flops=6 * slots_n * groups * width * units,
            bytes_accessed=6 * experts * width * units,
            transcendentals=0,
        ),
    )(first, *halves, gate_up, down)


def rms_scale(values, gain_vec):
    mean_sq = jnp.mean(values * values, axis=-1, keepdims=True)
    return values * lax.rsqrt(mean_sq + EPS) * gain_vec


def window_block(queries, key_rows, value_rows):
    scores = jnp.einsum(
        "qhgc,khc->hgqk", queries, key_rows, preferred_element_type=jnp.float32
    ) * HEAD_SIZE ** (-0.5)
    key_offset = jnp.arange(key_rows.shape[0])[None, :] - jnp.arange(queries.shape[0])[:, None]
    in_window = (key_offset >= 1) & (key_offset <= WINDOW_KEYS)
    scores = jnp.where(in_window, scores, -1e30)
    row_max = jnp.max(scores, axis=-1, keepdims=True)
    exponent = jnp.exp(scores - row_max)
    layer_weights = (exponent / jnp.sum(exponent, axis=-1, keepdims=True)).astype(jnp.bfloat16)
    attended = jnp.einsum(
        "hgqk,khc->qhgc", layer_weights, value_rows, preferred_element_type=jnp.float32
    )
    return attended.astype(jnp.bfloat16)


def local(
    stream_in,
    attn_gain,
    w_qkv,
    key_value_cache,
    w_out,
    mlp_gain,
    expert_index,
    gate_weight,
    w_gateup,
    w_down,
):
    seq_count = lax.axis_size("seq")
    tp_count = lax.axis_size("tp")
    length_local = stream_in.shape[0]
    heads_local = w_qkv.shape[1]
    query_group_width = QUERY_HEADS // KEY_VALUE_HEADS
    normed = rms_scale(stream_in.astype(jnp.float32), attn_gain).astype(jnp.bfloat16)
    projected_rows = jnp.einsum(
        "td,dhc->thc", normed, w_qkv, preferred_element_type=jnp.float32
    ).astype(jnp.bfloat16)
    projected_rows = projected_rows.reshape(
        length_local, heads_local, query_group_width + 2, HEAD_SIZE
    )
    queries = projected_rows[:, :, :query_group_width]
    kv_tail_rows = jnp.concatenate(
        [
            projected_rows[length_local - WINDOW_KEYS :, :, query_group_width],
            projected_rows[length_local - WINDOW_KEYS :, :, query_group_width + 1],
        ],
        axis=-1,
    )
    earlier = from_behind(kv_tail_rows, "seq", 1)
    at_start = lax.axis_index("seq") == 0
    earlier = jnp.where(at_start, key_value_cache, earlier)
    key_rows = jnp.concatenate(
        [earlier[:, :, :HEAD_SIZE], projected_rows[:, :, query_group_width]], axis=0
    )
    value_rows = jnp.concatenate(
        [earlier[:, :, HEAD_SIZE:], projected_rows[:, :, query_group_width + 1]], axis=0
    )
    attended = window_block(queries, key_rows, value_rows).reshape(
        length_local, heads_local * query_group_width * HEAD_SIZE
    )
    block_rows = length_local // tp_count
    plan = axis_plan(seq_count, tp_count)
    across = tp_count // 2

    terms = jnp.dot(attended, w_out, preferred_element_type=jnp.float32)
    terms = terms.reshape(across, 2, block_rows, MODEL_WIDTH)
    core = lax.axis_index("tp") % 2
    kept = lax.dynamic_index_in_dim(terms, core, 1, False)
    handed = lax.dynamic_index_in_dim(terms, 1 - core, 1, False).astype(jnp.bfloat16)
    kept = kept + swap(handed, 1, 1).astype(jnp.float32)
    place = lax.axis_index("tp") // 2
    attn_out = lax.dynamic_index_in_dim(kept, place, 0, False)
    for other in range(1, across):
        part = lax.dynamic_index_in_dim(kept, place ^ other, 0, False).astype(jnp.bfloat16)
        attn_out = attn_out + swap(part, 2 * other, 2 * other).astype(jnp.float32)
    own_start = lax.axis_index("tp") * block_rows
    residual = (
        lax.dynamic_slice_in_dim(stream_in, own_start, block_rows, 0).astype(jnp.float32) + attn_out
    )
    hidden_in = rms_scale(residual, mlp_gain).astype(jnp.bfloat16)

    experts_dev = w_gateup.shape[0]
    capacity = 2 * length_local * TOPK // (tp_count * EXPERTS)
    high = lax.reduce_precision(gate_weight, 8, 7)
    middle = lax.reduce_precision(gate_weight - high, 8, 7)
    low = lax.reduce_precision(gate_weight - high - middle, 8, 7)
    routing = jnp.concatenate([expert_index.astype(jnp.float32), high, middle, low], axis=1)
    routing = jnp.pad(routing, ((0, 0), (0, ROUTING - 4 * TOPK))).astype(jnp.bfloat16)
    rows = jnp.concatenate([hidden_in, routing], axis=1)

    (slow, slow_step, _), inner = plan[0], plan[1:]
    held = [rows] + [swap(rows, other * slow_step, other * slow_step) for other in range(1, slow)]
    mine = [join(spread(piece, inner)) for piece in held]
    halves = []
    for joined in mine:
        halves += [joined, swap(joined, 1, 1)]

    first = (lax.axis_index("seq") * experts_dev).astype(jnp.int32).reshape(1)
    weights = jnp.transpose(w_gateup, (0, 2, 3, 1))
    sums = run_experts(first, halves, weights, w_down, block_rows, capacity)

    total = residual
    for group in list(range(1, slow)) + [0]:
        kept, handed = sums[2 * group : 2 * group + 2]
        part = collect(kept, swap(handed, 1, 1), inner)
        if group:
            part = swap(part.astype(jnp.bfloat16), group * slow_step, group * slow_step)
        total = total + part[:, :MODEL_WIDTH].astype(jnp.float32)
    return total.astype(jnp.bfloat16)


def solution(mesh):
    in_specs = (
        P("seq", None),
        P(),
        P(None, "tp", None),
        P(None, "tp", None),
        P("tp", None),
        P(),
        P(("seq", "tp"), None),
        P(("seq", "tp"), None),
        P("seq", None, None, "tp"),
        P("seq", "tp", None),
    )
    out_specs = P(("seq", "tp"), None)
    return jax.shard_map(local, mesh=mesh, in_specs=in_specs, out_specs=out_specs, check_vma=False)
```

```python
import functools

import jax
import jax.numpy as jnp
from jax import lax
from jax.experimental import pallas as pl
from jax.experimental.pallas import tpu as pltpu
from jax.sharding import PartitionSpec as P

MODEL_WIDTH = 2880
QUERY_HEADS = 64
KEY_VALUE_HEADS = 8
HEAD_SIZE = 64
WINDOW_KEYS = 128
EXPERTS = 32
TOPK = 4


EPS = 1e-05


def from_behind(value, axis, steps):
    count = lax.axis_size(axis)
    first, last = (max(0, -steps), min(count, count - steps))
    return lax.ppermute(value, axis, [(source, source + steps) for source in range(first, last)])


def axis_plan(seq_count, tp_count):
    across = tp_count // 2
    slow = min(4, seq_count)
    quick = seq_count // slow
    x_step, quick_step, slow_step = 2, 2 * across, 2 * across * quick
    along = [(slow, slow_step, slow_step)]
    if across == quick:
        along.append((across, x_step, quick_step))
        along.append((across, quick_step, x_step))
    else:
        along.append((across, x_step, x_step))
        along.append((quick, quick_step, quick_step))
    return along


def swap(value, even_mask, odd_mask):
    count = lax.axis_size("seq") * lax.axis_size("tp")
    pairs = [
        (device, device ^ (odd_mask if device % 2 else even_mask)) for device in range(count)
    ]
    return lax.ppermute(value, ("seq", "tp"), pairs)


def spread(piece, steps):
    pieces = [piece]
    for size, even, odd in steps:
        pieces = pieces + [
            swap(held, other * even, other * odd) for other in range(1, size) for held in pieces
        ]
    return pieces


ROUTING = 64
SMALL_KERNEL = 8 << 20


def join_kernel(*refs):
    parts, out_ref = refs[:-1], refs[-1]
    rows = parts[0].shape[0]
    for place, part in enumerate(parts):
        out_ref[place * rows : (place + 1) * rows, :] = part[...]


def join(parts):
    rows, width = parts[0].shape
    return pl.pallas_call(
        join_kernel,
        out_shape=jax.ShapeDtypeStruct((len(parts) * rows, width), parts[0].dtype),
        compiler_params=pltpu.CompilerParams(vmem_limit_bytes=SMALL_KERNEL),
        cost_estimate=pl.CostEstimate(
            flops=0, bytes_accessed=4 * len(parts) * rows * width, transcendentals=0
        ),
    )(*parts)


def fold_kernel(count, *refs):
    terms, outs = refs[:count], refs[count:]
    rows = outs[0].shape[0]
    for place, out_ref in enumerate(outs):
        cut = slice(place * rows, (place + 1) * rows)
        total = terms[0][cut, :].astype(jnp.float32)
        for term in terms[1:]:
            total = total + term[cut, :].astype(jnp.float32)
        out_ref[...] = total.astype(out_ref.dtype)


def fold(terms, parts, first=jnp.float32):
    rows, width = terms[0].shape
    rows = rows // parts
    kinds = [first] + [jnp.bfloat16] * (parts - 1)
    return pl.pallas_call(
        functools.partial(fold_kernel, len(terms)),
        out_shape=[jax.ShapeDtypeStruct((rows, width), kind) for kind in kinds],
        compiler_params=pltpu.CompilerParams(vmem_limit_bytes=SMALL_KERNEL),
        cost_estimate=pl.CostEstimate(
            flops=len(terms) * rows * parts * width,
            bytes_accessed=4 * len(terms) * rows * parts * width,
            transcendentals=0,
        ),
    )(*terms)


def collect(kept, arrived, steps, last, first):
    terms = [kept, arrived]
    for size, even, odd in reversed(steps):
        parts = fold(terms, size)
        terms = [parts[0]] + [
            swap(parts[other], other * even, other * odd) for other in range(1, size)
        ]
    return fold(terms, last, first)


def expert_kernel(sizes, first_ref, *refs):
    groups, block_rows, capacity = sizes
    ins = refs[:groups]
    gate_up_ref, down_ref = refs[groups : groups + 2]
    outs = refs[groups + 2 : 2 * groups + 2]
    tokens_ref, gate_up_buf, down_buf, packed_ref, gate_ref, placer_ref = refs[2 * groups + 2 : -4]
    token_sem, gate_up_sem, down_sem, out_sem = refs[-4:]
    experts, _, units, width = gate_up_ref.shape
    tokens_n = ins[0].shape[0]
    per_group = tokens_n // block_rows
    span = per_group * capacity
    slots_n = experts * span

    def token_copy(group):
        return pltpu.make_async_copy(ins[group], tokens_ref.at[group], token_sem.at[group])

    def out_copy(group):
        return pltpu.make_async_copy(tokens_ref.at[group], outs[group], out_sem.at[group])

    def gate_up_copy(expert):
        return pltpu.make_async_copy(
            gate_up_ref.at[expert], gate_up_buf.at[expert % 2], gate_up_sem.at[expert % 2]
        )

    def down_copy(expert):
        return pltpu.make_async_copy(
            down_ref.at[expert], down_buf.at[expert % 2], down_sem.at[expert % 2]
        )

    for group in range(groups):
        token_copy(group).start()
    gate_up_copy(0).start()
    down_copy(0).start()

    slot = lax.broadcasted_iota(jnp.int32, (slots_n, tokens_n), 0)
    token = lax.broadcasted_iota(jnp.int32, (slots_n, tokens_n), 1)
    expert_of = (slot // span + first_ref[0]).astype(jnp.float32)
    place_of = (slot % capacity).astype(jnp.float32)
    own_block = (slot // capacity) % per_group == token // block_rows
    before = lax.broadcasted_iota(jnp.int32, (tokens_n, tokens_n), 0)
    after = lax.broadcasted_iota(jnp.int32, (tokens_n, tokens_n), 1)
    earlier = (before // block_rows == after // block_rows) & (before < after)
    earlier = jnp.where(earlier, 1.0, 0.0).astype(jnp.bfloat16)
    start = width + ROUTING - 128
    for group in range(groups):
        token_copy(group).wait()
        tail = tokens_ref[group, :, start : start + 128].astype(jnp.float32)
        tail = jnp.transpose(tail)[128 - ROUTING :]
        member = jnp.zeros((slots_n, tokens_n), jnp.float32)
        gate = jnp.zeros((slots_n, tokens_n), jnp.float32)
        for choice in range(TOPK):
            hit = tail[choice : choice + 1] == expert_of
            weight = (
                tail[TOPK + choice : TOPK + choice + 1]
                + tail[2 * TOPK + choice : 2 * TOPK + choice + 1]
                + tail[3 * TOPK + choice : 3 * TOPK + choice + 1]
            )
            member = member + jnp.where(hit, 1.0, 0.0)
            gate = gate + jnp.where(hit, weight, 0.0)
        rank = jnp.dot(member.astype(jnp.bfloat16), earlier, preferred_element_type=jnp.float32)
        chosen = own_block & (rank == place_of) & (member > 0.5)
        hot = jnp.where(chosen, 1.0, 0.0)
        gate = jnp.sum(jnp.where(chosen, gate, 0.0), axis=1, keepdims=True)
        placer_ref[group] = jnp.transpose(hot).astype(jnp.bfloat16)
        rows = tokens_ref[group, :, :width]
        packed = jnp.dot(hot.astype(jnp.bfloat16), rows, preferred_element_type=jnp.float32)
        packed = packed.astype(jnp.bfloat16)
        for expert in range(experts):
            place = slice(group * span, (group + 1) * span)
            packed_ref[expert, place] = packed[expert * span : (expert + 1) * span]
            gate_ref[expert, place] = jnp.broadcast_to(
                gate[expert * span : (expert + 1) * span], (span, 128)
            )

    contract = (((1,), (1,)), ((), ()))
    for expert in range(experts):
        held = expert % 2
        if expert + 1 < experts:
            gate_up_copy(expert + 1).start()
            down_copy(expert + 1).start()
        gate_up_copy(expert).wait()
        rows = packed_ref[expert]
        gate = lax.dot_general(
            rows, gate_up_buf[held, 0], contract, preferred_element_type=jnp.float32
        )
        up = lax.dot_general(
            rows, gate_up_buf[held, 1], contract, preferred_element_type=jnp.float32
        )
        act = gate / (1.0 + jnp.exp(-gate)) * up * gate_ref[expert][:, :1]
        act = act.astype(jnp.bfloat16)
        down_copy(expert).wait()
        result = jnp.dot(act, down_buf[held], preferred_element_type=jnp.float32)
        packed_ref[expert] = result.astype(jnp.bfloat16)

    for group in range(groups):
        place = slice(group * span, (group + 1) * span)
        rows = jnp.concatenate([packed_ref[expert, place] for expert in range(experts)], axis=0)
        summed = jnp.dot(placer_ref[group], rows, preferred_element_type=jnp.float32)
        tokens_ref[group, :, :width] = summed.astype(jnp.bfloat16)
        out_copy(group).start()
    for group in range(groups):
        out_copy(group).wait()


def run_experts(first, tokens, gate_up, down, block_rows, capacity):
    groups = len(tokens)
    tokens_n, wide = tokens[0].shape
    experts, _, units, width = gate_up.shape
    span = tokens_n // block_rows * capacity
    slots_n = experts * span
    anywhere = pl.BlockSpec(memory_space=pl.ANY)
    return pl.pallas_call(
        functools.partial(expert_kernel, (groups, block_rows, capacity)),
        in_specs=[pl.BlockSpec(memory_space=pltpu.SMEM)] + [anywhere] * (groups + 2),
        out_specs=[anywhere] * groups,
        out_shape=[jax.ShapeDtypeStruct((tokens_n, wide), jnp.bfloat16)] * groups,
        scratch_shapes=[
            pltpu.VMEM((groups, tokens_n, wide), jnp.bfloat16),
            pltpu.VMEM((2, 2, units, width), jnp.bfloat16),
            pltpu.VMEM((2, units, width), jnp.bfloat16),
            pltpu.VMEM((experts, groups * span, width), jnp.bfloat16),
            pltpu.VMEM((experts, groups * span, 128), jnp.float32),
            pltpu.VMEM((groups, tokens_n, slots_n), jnp.bfloat16),
            pltpu.SemaphoreType.DMA((groups,)),
            pltpu.SemaphoreType.DMA((2,)),
            pltpu.SemaphoreType.DMA((2,)),
            pltpu.SemaphoreType.DMA((groups,)),
        ],
        compiler_params=pltpu.CompilerParams(vmem_limit_bytes=52 << 20),
        cost_estimate=pl.CostEstimate(
            flops=6 * slots_n * groups * width * units,
            bytes_accessed=6 * experts * width * units,
            transcendentals=0,
        ),
    )(first, *tokens, gate_up, down)


def rms_scale(values, gain_vec):
    mean_sq = jnp.mean(values * values, axis=-1, keepdims=True)
    return values * lax.rsqrt(mean_sq + EPS) * gain_vec


def window_block(queries, key_rows, value_rows):
    scores = jnp.einsum(
        "qhgc,khc->hgqk", queries, key_rows, preferred_element_type=jnp.float32
    ) * HEAD_SIZE ** (-0.5)
    key_offset = jnp.arange(key_rows.shape[0])[None, :] - jnp.arange(queries.shape[0])[:, None]
    in_window = (key_offset >= 1) & (key_offset <= WINDOW_KEYS)
    scores = jnp.where(in_window, scores, -1e30)
    row_max = jnp.max(scores, axis=-1, keepdims=True)
    exponent = jnp.exp(scores - row_max)
    layer_weights = (exponent / jnp.sum(exponent, axis=-1, keepdims=True)).astype(jnp.bfloat16)
    attended = jnp.einsum(
        "hgqk,khc->qhgc", layer_weights, value_rows, preferred_element_type=jnp.float32
    )
    return attended.astype(jnp.bfloat16)


def local(
    stream_in,
    attn_gain,
    w_qkv,
    key_value_cache,
    w_out,
    mlp_gain,
    expert_index,
    gate_weight,
    w_gateup,
    w_down,
):
    seq_count = lax.axis_size("seq")
    tp_count = lax.axis_size("tp")
    length_local = stream_in.shape[0]
    heads_local = w_qkv.shape[1]
    query_group_width = QUERY_HEADS // KEY_VALUE_HEADS
    normed = rms_scale(stream_in.astype(jnp.float32), attn_gain).astype(jnp.bfloat16)
    projected_rows = jnp.einsum(
        "td,dhc->thc", normed, w_qkv, preferred_element_type=jnp.float32
    ).astype(jnp.bfloat16)
    projected_rows = projected_rows.reshape(
        length_local, heads_local, query_group_width + 2, HEAD_SIZE
    )
    queries = projected_rows[:, :, :query_group_width]
    kv_tail_rows = jnp.concatenate(
        [
            projected_rows[length_local - WINDOW_KEYS :, :, query_group_width],
            projected_rows[length_local - WINDOW_KEYS :, :, query_group_width + 1],
        ],
        axis=-1,
    )
    earlier = from_behind(kv_tail_rows, "seq", 1)
    at_start = lax.axis_index("seq") == 0
    earlier = jnp.where(at_start, key_value_cache, earlier)
    key_rows = jnp.concatenate(
        [earlier[:, :, :HEAD_SIZE], projected_rows[:, :, query_group_width]], axis=0
    )
    value_rows = jnp.concatenate(
        [earlier[:, :, HEAD_SIZE:], projected_rows[:, :, query_group_width + 1]], axis=0
    )
    attended = window_block(queries, key_rows, value_rows).reshape(
        length_local, heads_local * query_group_width * HEAD_SIZE
    )
    block_rows = length_local // tp_count
    plan = axis_plan(seq_count, tp_count)
    across = tp_count // 2

    terms = jnp.dot(attended, w_out, preferred_element_type=jnp.float32)
    terms = terms.reshape(across, 2, block_rows, MODEL_WIDTH)
    core = lax.axis_index("tp") % 2
    kept = lax.dynamic_index_in_dim(terms, core, 1, False)
    handed = lax.dynamic_index_in_dim(terms, 1 - core, 1, False).astype(jnp.bfloat16)
    kept = kept + swap(handed, 1, 1).astype(jnp.float32)
    place = lax.axis_index("tp") // 2
    attn_out = lax.dynamic_index_in_dim(kept, place, 0, False)
    for other in range(1, across):
        part = lax.dynamic_index_in_dim(kept, place ^ other, 0, False).astype(jnp.bfloat16)
        attn_out = attn_out + swap(part, 2 * other, 2 * other).astype(jnp.float32)
    own_start = lax.axis_index("tp") * block_rows
    residual = (
        lax.dynamic_slice_in_dim(stream_in, own_start, block_rows, 0).astype(jnp.float32) + attn_out
    )
    hidden_in = rms_scale(residual, mlp_gain).astype(jnp.bfloat16)

    experts_dev = w_gateup.shape[0]
    capacity = 2 * length_local * TOPK // (tp_count * EXPERTS)
    high = lax.reduce_precision(gate_weight, 8, 7)
    middle = lax.reduce_precision(gate_weight - high, 8, 7)
    low = lax.reduce_precision(gate_weight - high - middle, 8, 7)
    routing = jnp.concatenate([expert_index.astype(jnp.float32), high, middle, low], axis=1)
    routing = jnp.pad(routing, ((0, 0), (0, ROUTING - 4 * TOPK))).astype(jnp.bfloat16)
    rows = jnp.concatenate([hidden_in, routing], axis=1)

    (slow, slow_step, _), inner = plan[0], plan[1:]
    held = [rows] + [swap(rows, other * slow_step, other * slow_step) for other in range(1, slow)]
    near, far = held[: slow // 2], held[slow // 2 :]
    near, far = [join(spread(join(pieces), inner)) for pieces in (near, far)]
    tokens = [near, swap(near, 1, 1), far, swap(far, 1, 1)]

    first = (lax.axis_index("seq") * experts_dev).astype(jnp.int32).reshape(1)
    weights = jnp.transpose(w_gateup, (0, 2, 3, 1))
    near, near_handed, far, far_handed = run_experts(
        first, tokens, weights, w_down, block_rows, capacity
    )

    far = collect(far, swap(far_handed, 1, 1), inner, slow // 2, jnp.bfloat16)
    near = collect(near, swap(near_handed, 1, 1), inner, slow // 2, jnp.float32)
    total = residual + near[0][:, :MODEL_WIDTH]
    for other, part in enumerate(near[1:] + far, 1):
        part = swap(part, other * slow_step, other * slow_step)
        total = total + part[:, :MODEL_WIDTH].astype(jnp.float32)
    return total.astype(jnp.bfloat16)


def solution(mesh):
    in_specs = (
        P("seq", None),
        P(),
        P(None, "tp", None),
        P(None, "tp", None),
        P("tp", None),
        P(),
        P(("seq", "tp"), None),
        P(("seq", "tp"), None),
        P("seq", None, None, "tp"),
        P("seq", "tp", None),
    )
    out_specs = P(("seq", "tp"), None)
    return jax.shard_map(local, mesh=mesh, in_specs=in_specs, out_specs=out_specs, check_vma=False)
```

```python
import functools

import jax
import jax.numpy as jnp
from jax import lax
from jax.experimental import pallas as pl
from jax.experimental.pallas import tpu as pltpu
from jax.sharding import PartitionSpec as P

MODEL_WIDTH = 2880
QUERY_HEADS = 64
KEY_VALUE_HEADS = 8
HEAD_SIZE = 64
WINDOW_KEYS = 128
EXPERTS = 32
TOPK = 4


EPS = 1e-05


def from_behind(value, axis, steps):
    count = lax.axis_size(axis)
    first, last = (max(0, -steps), min(count, count - steps))
    return lax.ppermute(value, axis, [(source, source + steps) for source in range(first, last)])


def axis_plan(seq_count, tp_count):
    across = tp_count // 2
    slow = min(4, seq_count)
    quick = seq_count // slow
    x_step, quick_step, slow_step = 2, 2 * across, 2 * across * quick
    along = [(slow, slow_step, slow_step)]
    if across == quick:
        along.append((across, x_step, quick_step))
        along.append((across, quick_step, x_step))
    else:
        along.append((across, x_step, x_step))
        along.append((quick, quick_step, quick_step))
    return along


def swap(value, even_mask, odd_mask):
    count = lax.axis_size("seq") * lax.axis_size("tp")
    pairs = [
        (device, device ^ (odd_mask if device % 2 else even_mask)) for device in range(count)
    ]
    return lax.ppermute(value, ("seq", "tp"), pairs)


def spread(piece, steps):
    pieces = [piece]
    for size, even, odd in steps:
        pieces = pieces + [
            swap(held, other * even, other * odd) for other in range(1, size) for held in pieces
        ]
    return pieces


ROUTING = 64
SMALL_KERNEL = 8 << 20


def join_kernel(count, pieces, *refs):
    parts, out_ref = refs[:count], refs[-1]
    rows = parts[0].shape[0] // pieces
    for piece in range(pieces):
        for place, part in enumerate(parts):
            start = (piece * count + place) * rows
            out_ref[start : start + rows, :] = part[piece * rows : (piece + 1) * rows, :]


def join(parts, pieces=1, after=()):
    rows, width = parts[0].shape
    return pl.pallas_call(
        functools.partial(join_kernel, len(parts), pieces),
        in_specs=[pl.BlockSpec(memory_space=pltpu.VMEM)] * len(parts)
        + [pl.BlockSpec(memory_space=pl.ANY)] * len(after),
        out_shape=jax.ShapeDtypeStruct((len(parts) * rows, width), parts[0].dtype),
        compiler_params=pltpu.CompilerParams(vmem_limit_bytes=SMALL_KERNEL),
        cost_estimate=pl.CostEstimate(
            flops=0, bytes_accessed=4 * len(parts) * rows * width, transcendentals=0
        ),
    )(*parts, *after)


def fold_kernel(count, outs_n, *refs):
    terms, outs = refs[:count], refs[len(refs) - outs_n :]
    rows = outs[0].shape[0]
    for place, out_ref in enumerate(outs):
        cut = slice(place * rows, (place + 1) * rows)
        total = terms[0][cut, :].astype(jnp.float32)
        for term in terms[1:]:
            total = total + term[cut, :].astype(jnp.float32)
        out_ref[...] = total.astype(out_ref.dtype)


def fold(terms, kinds, after=()):
    rows, width = terms[0].shape
    rows = rows // len(kinds)
    return pl.pallas_call(
        functools.partial(fold_kernel, len(terms), len(kinds)),
        in_specs=[pl.BlockSpec(memory_space=pltpu.VMEM)] * len(terms)
        + [pl.BlockSpec(memory_space=pl.ANY)] * len(after),
        out_shape=[jax.ShapeDtypeStruct((rows, width), kind) for kind in kinds],
        compiler_params=pltpu.CompilerParams(vmem_limit_bytes=SMALL_KERNEL),
        cost_estimate=pl.CostEstimate(
            flops=len(terms) * rows * len(kinds) * width,
            bytes_accessed=4 * len(terms) * rows * len(kinds) * width,
            transcendentals=0,
        ),
    )(*terms, *after)


def send_parts(parts, even, odd):
    return [parts[0]] + [
        swap(part, other * even, other * odd) for other, part in enumerate(parts[1:], 1)
    ]


def expert_kernel(sizes, first_ref, *refs):
    groups, block_rows, capacity, lowest, experts, has_prior = sizes
    ins = refs[:groups]
    gate_up_ref, down_ref = refs[groups : groups + 2]
    priors = refs[groups + 2 : 2 * groups + 2] if has_prior else ()
    outs = refs[-groups - 11 : -11]
    tokens_ref, gate_up_buf, down_buf, packed_ref, gate_ref, placer_ref, prior_ref = refs[-11:-4]
    token_sem, gate_up_sem, down_sem, out_sem = refs[-4:]
    _, _, units, width = gate_up_ref.shape
    tokens_n = ins[0].shape[0]
    per_group = tokens_n // block_rows
    span = per_group * capacity
    slots_n = experts * span

    def token_copy(group):
        return pltpu.make_async_copy(ins[group], tokens_ref.at[group], token_sem.at[group])

    def out_copy(group):
        return pltpu.make_async_copy(tokens_ref.at[group], outs[group], out_sem.at[group])

    def prior_copy(group):
        return pltpu.make_async_copy(priors[group], prior_ref.at[group], out_sem.at[group])

    def gate_up_copy(expert, side):
        return pltpu.make_async_copy(
            gate_up_ref.at[lowest + expert, side],
            gate_up_buf.at[expert % 2, side],
            gate_up_sem.at[expert % 2, side],
        )

    def down_copy(expert):
        return pltpu.make_async_copy(
            down_ref.at[lowest + expert], down_buf.at[expert % 2], down_sem.at[expert % 2]
        )

    for group in range(groups):
        token_copy(group).start()
    for expert in range(min(2, experts)):
        gate_up_copy(expert, 0).start()
        gate_up_copy(expert, 1).start()
        down_copy(expert).start()
    for group in range(len(priors)):
        prior_copy(group).start()

    slot = lax.broadcasted_iota(jnp.int32, (slots_n, tokens_n), 0)
    token = lax.broadcasted_iota(jnp.int32, (slots_n, tokens_n), 1)
    expert_of = (slot // span + first_ref[0] + lowest).astype(jnp.float32)
    place_of = (slot % capacity).astype(jnp.float32)
    own_block = (slot // capacity) % per_group == token // block_rows
    before = lax.broadcasted_iota(jnp.int32, (tokens_n, tokens_n), 0)
    after = lax.broadcasted_iota(jnp.int32, (tokens_n, tokens_n), 1)
    earlier = (before // block_rows == after // block_rows) & (before < after)
    earlier = jnp.where(earlier, 1.0, 0.0).astype(jnp.bfloat16)
    start = width + ROUTING - 128
    for group in range(groups):
        token_copy(group).wait()
        tail = tokens_ref[group, :, start : start + 128].astype(jnp.float32)
        tail = jnp.transpose(tail)[128 - ROUTING :]
        member = jnp.zeros((slots_n, tokens_n), jnp.float32)
        gate = jnp.zeros((slots_n, tokens_n), jnp.float32)
        for choice in range(TOPK):
            hit = tail[choice : choice + 1] == expert_of
            weight = (
                tail[TOPK + choice : TOPK + choice + 1]
                + tail[2 * TOPK + choice : 2 * TOPK + choice + 1]
                + tail[3 * TOPK + choice : 3 * TOPK + choice + 1]
            )
            member = member + jnp.where(hit, 1.0, 0.0)
            gate = gate + jnp.where(hit, weight, 0.0)
        rank = jnp.dot(member.astype(jnp.bfloat16), earlier, preferred_element_type=jnp.float32)
        chosen = own_block & (rank == place_of) & (member > 0.5)
        hot = jnp.where(chosen, 1.0, 0.0)
        gate = jnp.sum(jnp.where(chosen, gate, 0.0), axis=1, keepdims=True)
        placer_ref[group] = jnp.transpose(hot).astype(jnp.bfloat16)
        rows = tokens_ref[group, :, :width]
        packed = jnp.dot(hot.astype(jnp.bfloat16), rows, preferred_element_type=jnp.float32)
        packed = packed.astype(jnp.bfloat16)
        for expert in range(experts):
            place = slice(group * span, (group + 1) * span)
            packed_ref[expert, place] = packed[expert * span : (expert + 1) * span]
            gate_ref[expert, place] = jnp.broadcast_to(
                gate[expert * span : (expert + 1) * span], (span, 128)
            )

    contract = (((1,), (1,)), ((), ()))
    for expert in range(experts):
        held = expert % 2
        rows = packed_ref[expert]
        gate_up_copy(expert, 0).wait()
        gate = lax.dot_general(
            rows, gate_up_buf[held, 0], contract, preferred_element_type=jnp.float32
        )
        gate_up_copy(expert, 1).wait()
        up = lax.dot_general(
            rows, gate_up_buf[held, 1], contract, preferred_element_type=jnp.float32
        )
        act = gate / (1.0 + jnp.exp(-gate)) * up * gate_ref[expert][:, :1]
        act = act.astype(jnp.bfloat16)
        down_copy(expert).wait()
        result = jnp.dot(act, down_buf[held], preferred_element_type=jnp.float32)
        packed_ref[expert] = result.astype(jnp.bfloat16)
        if expert + 2 < experts:
            gate_up_copy(expert + 2, 0).start()
            gate_up_copy(expert + 2, 1).start()
            down_copy(expert + 2).start()

    for group in range(groups):
        place = slice(group * span, (group + 1) * span)
        rows = jnp.concatenate([packed_ref[expert, place] for expert in range(experts)], axis=0)
        summed = jnp.dot(placer_ref[group], rows, preferred_element_type=jnp.float32)
        if has_prior:
            prior_copy(group).wait()
            summed = summed + prior_ref[group, :, :width].astype(jnp.float32)
        tokens_ref[group, :, :width] = summed.astype(jnp.bfloat16)
        out_copy(group).start()
    for group in range(groups):
        out_copy(group).wait()


def run_experts(first, tokens, gate_up, down, block_rows, capacity, part, prior=(), after=()):
    groups = len(tokens)
    tokens_n, wide = tokens[0].shape
    lowest, experts = part
    _, _, units, width = gate_up.shape
    span = tokens_n // block_rows * capacity
    slots_n = experts * span
    anywhere = pl.BlockSpec(memory_space=pl.ANY)
    return pl.pallas_call(
        functools.partial(
            expert_kernel, (groups, block_rows, capacity, lowest, experts, bool(prior))
        ),
        in_specs=[pl.BlockSpec(memory_space=pltpu.SMEM)] + [anywhere] * (groups + 2 + len(prior) + len(after)),
        out_specs=[anywhere] * groups,
        out_shape=[jax.ShapeDtypeStruct((tokens_n, wide), jnp.bfloat16)] * groups,
        scratch_shapes=[
            pltpu.VMEM((groups, tokens_n, wide), jnp.bfloat16),
            pltpu.VMEM((2, 2, units, width), jnp.bfloat16),
            pltpu.VMEM((2, units, width), jnp.bfloat16),
            pltpu.VMEM((experts, groups * span, width), jnp.bfloat16),
            pltpu.VMEM((experts, groups * span, 128), jnp.float32),
            pltpu.VMEM((groups, tokens_n, slots_n), jnp.bfloat16),
            pltpu.VMEM((groups if prior else 1, tokens_n if prior else 16, wide), jnp.bfloat16),
            pltpu.SemaphoreType.DMA((groups,)),
            pltpu.SemaphoreType.DMA((2, 2)),
            pltpu.SemaphoreType.DMA((2,)),
            pltpu.SemaphoreType.DMA((groups,)),
        ],
        compiler_params=pltpu.CompilerParams(vmem_limit_bytes=40 << 20),
        cost_estimate=pl.CostEstimate(
            flops=6 * slots_n * groups * width * units,
            bytes_accessed=6 * experts * width * units,
            transcendentals=0,
        ),
    )(first, *tokens, gate_up, down, *prior, *after)


def rms_scale(values, gain_vec):
    mean_sq = jnp.mean(values * values, axis=-1, keepdims=True)
    return values * lax.rsqrt(mean_sq + EPS) * gain_vec


def window_block(queries, key_rows, value_rows):
    scores = jnp.einsum(
        "qhgc,khc->hgqk", queries, key_rows, preferred_element_type=jnp.float32
    ) * HEAD_SIZE ** (-0.5)
    key_offset = jnp.arange(key_rows.shape[0])[None, :] - jnp.arange(queries.shape[0])[:, None]
    in_window = (key_offset >= 1) & (key_offset <= WINDOW_KEYS)
    scores = jnp.where(in_window, scores, -1e30)
    row_max = jnp.max(scores, axis=-1, keepdims=True)
    exponent = jnp.exp(scores - row_max)
    layer_weights = (exponent / jnp.sum(exponent, axis=-1, keepdims=True)).astype(jnp.bfloat16)
    attended = jnp.einsum(
        "hgqk,khc->qhgc", layer_weights, value_rows, preferred_element_type=jnp.float32
    )
    return attended.astype(jnp.bfloat16)


def local(
    stream_in,
    attn_gain,
    w_qkv,
    key_value_cache,
    w_out,
    mlp_gain,
    expert_index,
    gate_weight,
    w_gateup,
    w_down,
):
    seq_count = lax.axis_size("seq")
    tp_count = lax.axis_size("tp")
    length_local = stream_in.shape[0]
    heads_local = w_qkv.shape[1]
    query_group_width = QUERY_HEADS // KEY_VALUE_HEADS
    normed = rms_scale(stream_in.astype(jnp.float32), attn_gain).astype(jnp.bfloat16)
    projected_rows = jnp.einsum(
        "td,dhc->thc", normed, w_qkv, preferred_element_type=jnp.float32
    ).astype(jnp.bfloat16)
    projected_rows = projected_rows.reshape(
        length_local, heads_local, query_group_width + 2, HEAD_SIZE
    )
    queries = projected_rows[:, :, :query_group_width]
    kv_tail_rows = jnp.concatenate(
        [
            projected_rows[length_local - WINDOW_KEYS :, :, query_group_width],
            projected_rows[length_local - WINDOW_KEYS :, :, query_group_width + 1],
        ],
        axis=-1,
    )
    earlier = from_behind(kv_tail_rows, "seq", 1)
    at_start = lax.axis_index("seq") == 0
    earlier = jnp.where(at_start, key_value_cache, earlier)
    key_rows = jnp.concatenate(
        [earlier[:, :, :HEAD_SIZE], projected_rows[:, :, query_group_width]], axis=0
    )
    value_rows = jnp.concatenate(
        [earlier[:, :, HEAD_SIZE:], projected_rows[:, :, query_group_width + 1]], axis=0
    )
    attended = window_block(queries, key_rows, value_rows).reshape(
        length_local, heads_local * query_group_width * HEAD_SIZE
    )
    block_rows = length_local // tp_count
    plan = axis_plan(seq_count, tp_count)
    across = tp_count // 2

    terms = jnp.dot(attended, w_out, preferred_element_type=jnp.float32)
    terms = terms.reshape(across, 2, block_rows, MODEL_WIDTH)
    core = lax.axis_index("tp") % 2
    kept = lax.dynamic_index_in_dim(terms, core, 1, False)
    handed = lax.dynamic_index_in_dim(terms, 1 - core, 1, False).astype(jnp.bfloat16)
    kept = kept + swap(handed, 1, 1).astype(jnp.float32)
    place = lax.axis_index("tp") // 2
    attn_out = lax.dynamic_index_in_dim(kept, place, 0, False)
    for other in range(1, across):
        part = lax.dynamic_index_in_dim(kept, place ^ other, 0, False).astype(jnp.bfloat16)
        attn_out = attn_out + swap(part, 2 * other, 2 * other).astype(jnp.float32)
    own_start = lax.axis_index("tp") * block_rows
    residual = (
        lax.dynamic_slice_in_dim(stream_in, own_start, block_rows, 0).astype(jnp.float32) + attn_out
    )
    hidden_in = rms_scale(residual, mlp_gain).astype(jnp.bfloat16)

    experts_dev = w_gateup.shape[0]
    capacity = 2 * length_local * TOPK // (tp_count * EXPERTS)
    high = lax.reduce_precision(gate_weight, 8, 7)
    middle = lax.reduce_precision(gate_weight - high, 8, 7)
    low = lax.reduce_precision(gate_weight - high - middle, 8, 7)
    routing = jnp.concatenate([expert_index.astype(jnp.float32), high, middle, low], axis=1)
    routing = jnp.pad(routing, ((0, 0), (0, ROUTING - 4 * TOPK))).astype(jnp.bfloat16)
    rows = jnp.concatenate([hidden_in, routing], axis=1)

    (slow, slow_step, _), inner = plan[0], plan[1:]
    last = inner[-1]
    half = slow // 2

    def along(value, offset):
        return swap(value, offset * slow_step, offset * slow_step)

    even_pieces = [rows] + [along(rows, offset) for offset in range(2, slow, 2)]
    odd_pieces = [along(rows, 1)]
    odd_pieces += [along(join([rows], 1, even_pieces[1:]), offset) for offset in range(3, slow, 2)]
    pair = join(odd_pieces)
    pieces_a = [piece for start in even_pieces for piece in spread(start, inner)]
    mine_a = join(pieces_a, 1, (pair,))
    tokens_a = [mine_a, swap(mine_a, 1, 1)]

    first = (lax.axis_index("seq") * experts_dev).astype(jnp.int32).reshape(1)
    weights = (jnp.transpose(w_gateup, (0, 2, 3, 1)), w_down, block_rows, capacity)
    cut = experts_dev // 2
    lower, upper = (0, cut), (cut, experts_dev - cut)

    (size, even, odd), (last_size, last_even, last_odd) = inner
    near = [swap(pair, other * even, other * odd) for other in range(1, size)]
    far = [swap(pair, other * last_even, other * last_odd) for other in range(1, last_size)]
    sums_a = run_experts(first, tokens_a, *weights, lower)
    passed = [join([piece], 1, sums_a[:1]) for piece in near]
    pieces_b = [pair] + near
    for other, piece in enumerate(far, 1):
        pieces_b += [piece]
        pieces_b += [swap(held, other * last_even, other * last_odd) for held in passed]
    sums_a = run_experts(first, tokens_a, *weights, upper, sums_a)
    mine_b = join(pieces_b, half)
    tokens_b = [mine_b, swap(mine_b, 1, 1)]

    kinds = ([jnp.float32] + [jnp.bfloat16] * (last_size - 1)) * half

    def send_back(sums, after=()):
        parts = fold([sums[0], swap(sums[1], 1, 1)], kinds, after)
        return [
            send_parts(parts[place : place + last_size], last_even, last_odd)
            for place in range(0, half * last_size, last_size)
        ]

    terms_a = send_back(sums_a)
    sums_b = run_experts(first, tokens_b, *weights, lower)
    size, even, odd = inner[0]
    inner_kinds = [jnp.float32] + [jnp.bfloat16] * (size - 1)
    halfway = [fold(terms, inner_kinds, sums_b[:1]) for terms in terms_a]
    sums_b = run_experts(
        first, tokens_b, *weights, upper, sums_b, [parts[0] for parts in halfway]
    )
    terms_a = [send_parts(parts, even, odd) for parts in halfway]
    own = fold(terms_a[0], [jnp.float32])[0]
    parts_a = [fold(terms, [jnp.bfloat16])[0] for terms in terms_a[1:]]
    arrived = [along(part, 2 * piece) for piece, part in enumerate(parts_a, 1)]

    terms_b = send_back(sums_b, [own] + parts_a)
    after = ()
    before_last = tuple(arrived)
    for piece in reversed(range(half)):
        terms = send_parts(fold(terms_b[piece], inner_kinds, after), even, odd)
        part = fold(terms, [jnp.bfloat16], before_last)[0]
        after, before_last = (part,), ()
        arrived.append(along(part, 2 * piece + 1))
    total = residual + own[:, :MODEL_WIDTH]
    for part in arrived:
        total = total + part[:, :MODEL_WIDTH].astype(jnp.float32)
    return total.astype(jnp.bfloat16)


def solution(mesh):
    in_specs = (
        P("seq", None),
        P(),
        P(None, "tp", None),
        P(None, "tp", None),
        P("tp", None),
        P(),
        P(("seq", "tp"), None),
        P(("seq", "tp"), None),
        P("seq", None, None, "tp"),
        P("seq", "tp", None),
    )
    out_specs = P(("seq", "tp"), None)
    return jax.shard_map(local, mesh=mesh, in_specs=in_specs, out_specs=out_specs, check_vma=False)
```

```python
import functools

import jax
import jax.numpy as jnp
from jax import lax
from jax.experimental import pallas as pl
from jax.experimental.pallas import tpu as pltpu
from jax.sharding import PartitionSpec as P

MODEL_WIDTH = 2880
QUERY_HEADS = 64
KEY_VALUE_HEADS = 8
HEAD_SIZE = 64
WINDOW_KEYS = 128
EXPERTS = 32
TOPK = 4


EPS = 1e-05


def from_behind(value, axis, steps):
    count = lax.axis_size(axis)
    first, last = (max(0, -steps), min(count, count - steps))
    return lax.ppermute(value, axis, [(source, source + steps) for source in range(first, last)])


def axis_plan(seq_count, tp_count):
    across = tp_count // 2
    slow = min(4, seq_count)
    quick = seq_count // slow
    x_step, quick_step, slow_step = 2, 2 * across, 2 * across * quick
    along = [(slow, slow_step, slow_step)]
    if across == quick:
        along.append((across, x_step, quick_step))
        along.append((across, quick_step, x_step))
    else:
        along.append((across, x_step, x_step))
        along.append((quick, quick_step, quick_step))
    return along


def swap(value, even_mask, odd_mask):
    count = lax.axis_size("seq") * lax.axis_size("tp")
    pairs = [
        (device, device ^ (odd_mask if device % 2 else even_mask)) for device in range(count)
    ]
    return lax.ppermute(value, ("seq", "tp"), pairs)


def spread(piece, steps):
    pieces = [piece]
    for size, even, odd in steps:
        pieces = pieces + [
            swap(held, other * even, other * odd) for other in range(1, size) for held in pieces
        ]
    return pieces


ROUTING = 64
SMALL_KERNEL = 8 << 20
WEIGHT_PIECES = 4


def join_kernel(count, pieces, *refs):
    parts, out_ref = refs[:count], refs[-1]
    rows = parts[0].shape[0] // pieces
    for piece in range(pieces):
        for place, part in enumerate(parts):
            start = (piece * count + place) * rows
            out_ref[start : start + rows, :] = part[piece * rows : (piece + 1) * rows, :]


def join(parts, pieces=1, after=()):
    rows, width = parts[0].shape
    return pl.pallas_call(
        functools.partial(join_kernel, len(parts), pieces),
        in_specs=[pl.BlockSpec(memory_space=pltpu.VMEM)] * len(parts)
        + [pl.BlockSpec(memory_space=pl.ANY)] * len(after),
        out_shape=jax.ShapeDtypeStruct((len(parts) * rows, width), parts[0].dtype),
        compiler_params=pltpu.CompilerParams(vmem_limit_bytes=SMALL_KERNEL),
        cost_estimate=pl.CostEstimate(
            flops=0, bytes_accessed=4 * len(parts) * rows * width, transcendentals=0
        ),
    )(*parts, *after)


def fold_kernel(count, outs_n, *refs):
    terms, outs = refs[:count], refs[len(refs) - outs_n :]
    rows = outs[0].shape[0]
    for place, out_ref in enumerate(outs):
        cut = slice(place * rows, (place + 1) * rows)
        total = terms[0][cut, :].astype(jnp.float32)
        for term in terms[1:]:
            total = total + term[cut, :].astype(jnp.float32)
        out_ref[...] = total.astype(out_ref.dtype)


def fold(terms, kinds, after=()):
    rows, width = terms[0].shape
    rows = rows // len(kinds)
    return pl.pallas_call(
        functools.partial(fold_kernel, len(terms), len(kinds)),
        in_specs=[pl.BlockSpec(memory_space=pltpu.VMEM)] * len(terms)
        + [pl.BlockSpec(memory_space=pl.ANY)] * len(after),
        out_shape=[jax.ShapeDtypeStruct((rows, width), kind) for kind in kinds],
        compiler_params=pltpu.CompilerParams(vmem_limit_bytes=SMALL_KERNEL),
        cost_estimate=pl.CostEstimate(
            flops=len(terms) * rows * len(kinds) * width,
            bytes_accessed=4 * len(terms) * rows * len(kinds) * width,
            transcendentals=0,
        ),
    )(*terms, *after)


def send_parts(parts, even, odd):
    return [parts[0]] + [
        swap(part, other * even, other * odd) for other, part in enumerate(parts[1:], 1)
    ]


def expert_kernel(sizes, first_ref, *refs):
    groups, block_rows, capacity, lowest, experts, has_prior = sizes
    ins = refs[:groups]
    gate_up_ref, down_ref = refs[groups : groups + 2]
    priors = refs[groups + 2 : 2 * groups + 2] if has_prior else ()
    outs = refs[-groups - 10 : -10]
    tokens_ref, gate_up_buf, down_buf, packed_ref, gate_ref, placer_ref, prior_ref = refs[-10:-3]
    token_sem, weight_sem, out_sem = refs[-3:]
    _, _, units, width = gate_up_ref.shape
    tokens_n = ins[0].shape[0]
    per_group = tokens_n // block_rows
    span = per_group * capacity
    slots_n = experts * span

    def token_copy(group):
        return pltpu.make_async_copy(ins[group], tokens_ref.at[group], token_sem.at[group])

    def out_copy(group):
        return pltpu.make_async_copy(tokens_ref.at[group], outs[group], out_sem.at[group])

    def prior_copy(group):
        return pltpu.make_async_copy(priors[group], prior_ref.at[group], out_sem.at[group])

    step = units // 3 if units % 48 == 0 else units
    per_matrix = units // step
    pieces = [
        (expert, matrix, start)
        for expert in range(experts)
        for matrix in range(3)
        for start in range(0, units, step)
    ]

    def weight_copy(number):
        expert, matrix, start = pieces[number]
        rows = pl.ds(start, step)
        if matrix == 2:
            source = down_ref.at[lowest + expert, rows]
            target = down_buf.at[expert % 2, rows]
        else:
            source = gate_up_ref.at[lowest + expert, matrix, rows]
            target = gate_up_buf.at[expert % 2, matrix, rows]
        return pltpu.make_async_copy(source, target, weight_sem.at[number % WEIGHT_PIECES])

    def weights_ready(expert, matrix):
        first = (expert * 3 + matrix) * per_matrix
        for number in range(first, first + per_matrix):
            weight_copy(number).wait()
            if number + WEIGHT_PIECES < len(pieces):
                weight_copy(number + WEIGHT_PIECES).start()

    for group in range(groups):
        token_copy(group).start()
    for number in range(min(WEIGHT_PIECES, len(pieces))):
        weight_copy(number).start()
    for group in range(len(priors)):
        prior_copy(group).start()

    slot = lax.broadcasted_iota(jnp.int32, (slots_n, tokens_n), 0)
    token = lax.broadcasted_iota(jnp.int32, (slots_n, tokens_n), 1)
    expert_of = (slot // span + first_ref[0] + lowest).astype(jnp.float32)
    place_of = (slot % capacity).astype(jnp.float32)
    own_block = (slot // capacity) % per_group == token // block_rows
    before = lax.broadcasted_iota(jnp.int32, (tokens_n, tokens_n), 0)
    after = lax.broadcasted_iota(jnp.int32, (tokens_n, tokens_n), 1)
    earlier = (before // block_rows == after // block_rows) & (before < after)
    earlier = jnp.where(earlier, 1.0, 0.0).astype(jnp.bfloat16)
    start = width + ROUTING - 128
    for group in range(groups):
        token_copy(group).wait()
        tail = tokens_ref[group, :, start : start + 128].astype(jnp.float32)
        tail = jnp.transpose(tail)[128 - ROUTING :]
        member = jnp.zeros((slots_n, tokens_n), jnp.float32)
        gate = jnp.zeros((slots_n, tokens_n), jnp.float32)
        for choice in range(TOPK):
            hit = tail[choice : choice + 1] == expert_of
            weight = (
                tail[TOPK + choice : TOPK + choice + 1]
                + tail[2 * TOPK + choice : 2 * TOPK + choice + 1]
                + tail[3 * TOPK + choice : 3 * TOPK + choice + 1]
            )
            member = member + jnp.where(hit, 1.0, 0.0)
            gate = gate + jnp.where(hit, weight, 0.0)
        rank = jnp.dot(member.astype(jnp.bfloat16), earlier, preferred_element_type=jnp.float32)
        chosen = own_block & (rank == place_of) & (member > 0.5)
        hot = jnp.where(chosen, 1.0, 0.0)
        gate = jnp.sum(jnp.where(chosen, gate, 0.0), axis=1, keepdims=True)
        placer_ref[group] = jnp.transpose(hot).astype(jnp.bfloat16)
        rows = tokens_ref[group, :, :width]
        packed = jnp.dot(hot.astype(jnp.bfloat16), rows, preferred_element_type=jnp.float32)
        packed = packed.astype(jnp.bfloat16)
        for expert in range(experts):
            place = slice(group * span, (group + 1) * span)
            packed_ref[expert, place] = packed[expert * span : (expert + 1) * span]
            gate_ref[expert, place] = jnp.broadcast_to(
                gate[expert * span : (expert + 1) * span], (span, 128)
            )

    contract = (((1,), (1,)), ((), ()))
    for expert in range(experts):
        held = expert % 2
        rows = packed_ref[expert]
        weights_ready(expert, 0)
        gate = lax.dot_general(
            rows, gate_up_buf[held, 0], contract, preferred_element_type=jnp.float32
        )
        weights_ready(expert, 1)
        up = lax.dot_general(
            rows, gate_up_buf[held, 1], contract, preferred_element_type=jnp.float32
        )
        act = gate / (1.0 + jnp.exp(-gate)) * up * gate_ref[expert][:, :1]
        act = act.astype(jnp.bfloat16)
        weights_ready(expert, 2)
        result = jnp.dot(act, down_buf[held], preferred_element_type=jnp.float32)
        packed_ref[expert] = result.astype(jnp.bfloat16)

    for group in range(groups):
        place = slice(group * span, (group + 1) * span)
        rows = jnp.concatenate([packed_ref[expert, place] for expert in range(experts)], axis=0)
        summed = jnp.dot(placer_ref[group], rows, preferred_element_type=jnp.float32)
        if has_prior:
            prior_copy(group).wait()
            summed = summed + prior_ref[group, :, :width].astype(jnp.float32)
        tokens_ref[group, :, :width] = summed.astype(jnp.bfloat16)
        out_copy(group).start()
    for group in range(groups):
        out_copy(group).wait()


def run_experts(first, tokens, gate_up, down, block_rows, capacity, part, prior=(), after=()):
    groups = len(tokens)
    tokens_n, wide = tokens[0].shape
    lowest, experts = part
    _, _, units, width = gate_up.shape
    span = tokens_n // block_rows * capacity
    slots_n = experts * span
    anywhere = pl.BlockSpec(memory_space=pl.ANY)
    return pl.pallas_call(
        functools.partial(
            expert_kernel, (groups, block_rows, capacity, lowest, experts, bool(prior))
        ),
        in_specs=[pl.BlockSpec(memory_space=pltpu.SMEM)] + [anywhere] * (groups + 2 + len(prior) + len(after)),
        out_specs=[anywhere] * groups,
        out_shape=[jax.ShapeDtypeStruct((tokens_n, wide), jnp.bfloat16)] * groups,
        scratch_shapes=[
            pltpu.VMEM((groups, tokens_n, wide), jnp.bfloat16),
            pltpu.VMEM((2, 2, units, width), jnp.bfloat16),
            pltpu.VMEM((2, units, width), jnp.bfloat16),
            pltpu.VMEM((experts, groups * span, width), jnp.bfloat16),
            pltpu.VMEM((experts, groups * span, 128), jnp.float32),
            pltpu.VMEM((groups, tokens_n, slots_n), jnp.bfloat16),
            pltpu.VMEM((groups if prior else 1, tokens_n if prior else 16, wide), jnp.bfloat16),
            pltpu.SemaphoreType.DMA((groups,)),
            pltpu.SemaphoreType.DMA((WEIGHT_PIECES,)),
            pltpu.SemaphoreType.DMA((groups,)),
        ],
        compiler_params=pltpu.CompilerParams(vmem_limit_bytes=40 << 20),
        cost_estimate=pl.CostEstimate(
            flops=6 * slots_n * groups * width * units,
            bytes_accessed=6 * experts * width * units,
            transcendentals=0,
        ),
    )(first, *tokens, gate_up, down, *prior, *after)


def rms_scale(values, gain_vec):
    mean_sq = jnp.mean(values * values, axis=-1, keepdims=True)
    return values * lax.rsqrt(mean_sq + EPS) * gain_vec


def window_block(queries, key_rows, value_rows):
    scores = jnp.einsum(
        "qhgc,khc->hgqk", queries, key_rows, preferred_element_type=jnp.float32
    ) * HEAD_SIZE ** (-0.5)
    key_offset = jnp.arange(key_rows.shape[0])[None, :] - jnp.arange(queries.shape[0])[:, None]
    in_window = (key_offset >= 1) & (key_offset <= WINDOW_KEYS)
    scores = jnp.where(in_window, scores, -1e30)
    row_max = jnp.max(scores, axis=-1, keepdims=True)
    exponent = jnp.exp(scores - row_max)
    layer_weights = (exponent / jnp.sum(exponent, axis=-1, keepdims=True)).astype(jnp.bfloat16)
    attended = jnp.einsum(
        "hgqk,khc->qhgc", layer_weights, value_rows, preferred_element_type=jnp.float32
    )
    return attended.astype(jnp.bfloat16)


def local(
    stream_in,
    attn_gain,
    w_qkv,
    key_value_cache,
    w_out,
    mlp_gain,
    expert_index,
    gate_weight,
    w_gateup,
    w_down,
):
    seq_count = lax.axis_size("seq")
    tp_count = lax.axis_size("tp")
    length_local = stream_in.shape[0]
    heads_local = w_qkv.shape[1]
    query_group_width = QUERY_HEADS // KEY_VALUE_HEADS
    normed = rms_scale(stream_in.astype(jnp.float32), attn_gain).astype(jnp.bfloat16)
    projected_rows = jnp.einsum(
        "td,dhc->thc", normed, w_qkv, preferred_element_type=jnp.float32
    ).astype(jnp.bfloat16)
    projected_rows = projected_rows.reshape(
        length_local, heads_local, query_group_width + 2, HEAD_SIZE
    )
    queries = projected_rows[:, :, :query_group_width]
    kv_tail_rows = jnp.concatenate(
        [
            projected_rows[length_local - WINDOW_KEYS :, :, query_group_width],
            projected_rows[length_local - WINDOW_KEYS :, :, query_group_width + 1],
        ],
        axis=-1,
    )
    earlier = from_behind(kv_tail_rows, "seq", 1)
    at_start = lax.axis_index("seq") == 0
    earlier = jnp.where(at_start, key_value_cache, earlier)
    key_rows = jnp.concatenate(
        [earlier[:, :, :HEAD_SIZE], projected_rows[:, :, query_group_width]], axis=0
    )
    value_rows = jnp.concatenate(
        [earlier[:, :, HEAD_SIZE:], projected_rows[:, :, query_group_width + 1]], axis=0
    )
    attended = window_block(queries, key_rows, value_rows).reshape(
        length_local, heads_local * query_group_width * HEAD_SIZE
    )
    block_rows = length_local // tp_count
    plan = axis_plan(seq_count, tp_count)
    across = tp_count // 2

    terms = jnp.dot(attended, w_out, preferred_element_type=jnp.float32)
    terms = terms.reshape(across, 2, block_rows, MODEL_WIDTH)
    core = lax.axis_index("tp") % 2
    kept = lax.dynamic_index_in_dim(terms, core, 1, False)
    handed = lax.dynamic_index_in_dim(terms, 1 - core, 1, False).astype(jnp.bfloat16)
    kept = kept + swap(handed, 1, 1).astype(jnp.float32)
    place = lax.axis_index("tp") // 2
    attn_out = lax.dynamic_index_in_dim(kept, place, 0, False)
    for other in range(1, across):
        part = lax.dynamic_index_in_dim(kept, place ^ other, 0, False).astype(jnp.bfloat16)
        attn_out = attn_out + swap(part, 2 * other, 2 * other).astype(jnp.float32)
    own_start = lax.axis_index("tp") * block_rows
    residual = (
        lax.dynamic_slice_in_dim(stream_in, own_start, block_rows, 0).astype(jnp.float32) + attn_out
    )
    hidden_in = rms_scale(residual, mlp_gain).astype(jnp.bfloat16)

    experts_dev = w_gateup.shape[0]
    capacity = 2 * length_local * TOPK // (tp_count * EXPERTS)
    high = lax.reduce_precision(gate_weight, 8, 7)
    middle = lax.reduce_precision(gate_weight - high, 8, 7)
    low = lax.reduce_precision(gate_weight - high - middle, 8, 7)
    routing = jnp.concatenate([expert_index.astype(jnp.float32), high, middle, low], axis=1)
    routing = jnp.pad(routing, ((0, 0), (0, ROUTING - 4 * TOPK))).astype(jnp.bfloat16)
    rows = jnp.concatenate([hidden_in, routing], axis=1)

    (slow, slow_step, _), inner = plan[0], plan[1:]
    last = inner[-1]
    half = slow // 2

    def along(value, offset):
        return swap(value, offset * slow_step, offset * slow_step)

    even_pieces = [rows] + [along(rows, offset) for offset in range(2, slow, 2)]
    odd_pieces = [along(rows, 1)]
    odd_pieces += [along(join([rows], 1, even_pieces[1:]), offset) for offset in range(3, slow, 2)]
    pair = join(odd_pieces)
    pieces_a = [piece for start in even_pieces for piece in spread(start, inner)]
    mine_a = join(pieces_a, 1, (pair,))
    tokens_a = [mine_a, swap(mine_a, 1, 1)]

    first = (lax.axis_index("seq") * experts_dev).astype(jnp.int32).reshape(1)
    weights = (jnp.transpose(w_gateup, (0, 2, 3, 1)), w_down, block_rows, capacity)
    cut = experts_dev // 2
    lower, upper = (0, cut), (cut, experts_dev - cut)

    (size, even, odd), (last_size, last_even, last_odd) = inner
    near = [swap(pair, other * even, other * odd) for other in range(1, size)]
    far = [swap(pair, other * last_even, other * last_odd) for other in range(1, last_size)]
    sums_a = run_experts(first, tokens_a, *weights, lower)
    passed = [join([piece], 1, sums_a[:1]) for piece in near]
    pieces_b = [pair] + near
    for other, piece in enumerate(far, 1):
        pieces_b += [piece]
        pieces_b += [swap(held, other * last_even, other * last_odd) for held in passed]
    sums_a = run_experts(first, tokens_a, *weights, upper, sums_a)
    mine_b = join(pieces_b, half)
    tokens_b = [mine_b, swap(mine_b, 1, 1)]

    kinds = ([jnp.float32] + [jnp.bfloat16] * (last_size - 1)) * half

    def send_back(sums, after=()):
        parts = fold([sums[0], swap(sums[1], 1, 1)], kinds, after)
        return [
            send_parts(parts[place : place + last_size], last_even, last_odd)
            for place in range(0, half * last_size, last_size)
        ]

    terms_a = send_back(sums_a)
    quarter = max(1, cut // 2)
    stages = [(0, quarter), (quarter, experts_dev - 2 * quarter), (experts_dev - quarter, quarter)]
    stages = [stage for stage in stages if stage[1]]
    sums_b = run_experts(first, tokens_b, *weights, stages[0])
    size, even, odd = inner[0]
    inner_kinds = [jnp.float32] + [jnp.bfloat16] * (size - 1)
    halfway = [fold(terms, inner_kinds, sums_b[:1]) for terms in terms_a]
    terms_a = [send_parts(parts, even, odd) for parts in halfway]
    marks = [parts[0] for parts in halfway]
    for place, stage in enumerate(stages[1:]):
        sums_b = run_experts(first, tokens_b, *weights, stage, sums_b, marks)
        if place == 0:
            own = fold(terms_a[0], [jnp.float32], sums_b[:1])[0]
            parts_a = [fold(terms, [jnp.bfloat16], sums_b[:1])[0] for terms in terms_a[1:]]
            arrived = [along(part, 2 * piece) for piece, part in enumerate(parts_a, 1)]
            marks = [own] + parts_a

    terms_b = send_back(sums_b)
    after = ()
    before_last = tuple(arrived)
    for piece in reversed(range(half)):
        terms = send_parts(fold(terms_b[piece], inner_kinds, after), even, odd)
        part = fold(terms, [jnp.bfloat16], before_last)[0]
        after, before_last = (part,), ()
        arrived.append(along(part, 2 * piece + 1))
    total = residual + own[:, :MODEL_WIDTH]
    for part in arrived:
        total = total + part[:, :MODEL_WIDTH].astype(jnp.float32)
    return total.astype(jnp.bfloat16)


def solution(mesh):
    in_specs = (
        P("seq", None),
        P(),
        P(None, "tp", None),
        P(None, "tp", None),
        P("tp", None),
        P(),
        P(("seq", "tp"), None),
        P(("seq", "tp"), None),
        P("seq", None, None, "tp"),
        P("seq", "tp", None),
    )
    out_specs = P(("seq", "tp"), None)
    return jax.shard_map(local, mesh=mesh, in_specs=in_specs, out_specs=out_specs, check_vma=False)
```

```python
import functools

import jax
import jax.numpy as jnp
from jax import lax
from jax.experimental import pallas as pl
from jax.experimental.pallas import tpu as pltpu
from jax.sharding import PartitionSpec as P

MODEL_WIDTH = 2880
QUERY_HEADS = 64
KEY_VALUE_HEADS = 8
HEAD_SIZE = 64
WINDOW_KEYS = 128
EXPERTS = 32
TOPK = 4


EPS = 1e-05


def from_behind(value, axis, steps):
    count = lax.axis_size(axis)
    first, last = (max(0, -steps), min(count, count - steps))
    return lax.ppermute(value, axis, [(source, source + steps) for source in range(first, last)])


def axis_plan(seq_count, tp_count):
    across = tp_count // 2
    slow = min(4, seq_count)
    quick = seq_count // slow
    x_step, quick_step, slow_step = 2, 2 * across, 2 * across * quick
    along = [(slow, slow_step, slow_step)]
    if across == quick:
        along.append((across, x_step, quick_step))
        along.append((across, quick_step, x_step))
    else:
        along.append((across, x_step, x_step))
        along.append((quick, quick_step, quick_step))
    return along


def swap(value, even_mask, odd_mask):
    count = lax.axis_size("seq") * lax.axis_size("tp")
    pairs = [
        (device, device ^ (odd_mask if device % 2 else even_mask)) for device in range(count)
    ]
    return lax.ppermute(value, ("seq", "tp"), pairs)


def spread(piece, steps):
    pieces = [piece]
    for size, even, odd in steps:
        pieces = pieces + [
            swap(held, other * even, other * odd) for other in range(1, size) for held in pieces
        ]
    return pieces


ROUTING = 64
SMALL_KERNEL = 8 << 20
EXPERT_KERNEL = 6 << 20


def join_kernel(count, pieces, *refs):
    parts, out_ref = refs[:count], refs[-1]
    rows = parts[0].shape[0] // pieces
    for piece in range(pieces):
        for place, part in enumerate(parts):
            start = (piece * count + place) * rows
            out_ref[start : start + rows, :] = part[piece * rows : (piece + 1) * rows, :]


def join(parts, pieces=1, after=()):
    rows, width = parts[0].shape
    return pl.pallas_call(
        functools.partial(join_kernel, len(parts), pieces),
        in_specs=[pl.BlockSpec(memory_space=pltpu.VMEM)] * len(parts)
        + [pl.BlockSpec(memory_space=pl.ANY)] * len(after),
        out_shape=jax.ShapeDtypeStruct((len(parts) * rows, width), parts[0].dtype),
        compiler_params=pltpu.CompilerParams(vmem_limit_bytes=SMALL_KERNEL),
        cost_estimate=pl.CostEstimate(
            flops=0, bytes_accessed=4 * len(parts) * rows * width, transcendentals=0
        ),
    )(*parts, *after)


def fold_kernel(count, outs_n, *refs):
    terms, outs = refs[:count], refs[len(refs) - outs_n :]
    rows = outs[0].shape[0]
    for place, out_ref in enumerate(outs):
        cut = slice(place * rows, (place + 1) * rows)
        total = terms[0][cut, :].astype(jnp.float32)
        for term in terms[1:]:
            total = total + term[cut, :].astype(jnp.float32)
        out_ref[...] = total.astype(out_ref.dtype)


def fold(terms, kinds, after=()):
    rows, width = terms[0].shape
    rows = rows // len(kinds)
    return pl.pallas_call(
        functools.partial(fold_kernel, len(terms), len(kinds)),
        in_specs=[pl.BlockSpec(memory_space=pltpu.VMEM)] * len(terms)
        + [pl.BlockSpec(memory_space=pl.ANY)] * len(after),
        out_shape=[jax.ShapeDtypeStruct((rows, width), kind) for kind in kinds],
        compiler_params=pltpu.CompilerParams(vmem_limit_bytes=SMALL_KERNEL),
        cost_estimate=pl.CostEstimate(
            flops=len(terms) * rows * len(kinds) * width,
            bytes_accessed=4 * len(terms) * rows * len(kinds) * width,
            transcendentals=0,
        ),
    )(*terms, *after)


def send_parts(parts, even, odd):
    return [parts[0]] + [
        swap(part, other * even, other * odd) for other, part in enumerate(parts[1:], 1)
    ]


PIECE_ROWS = 256
PIECE_SLOTS = 6
COLUMNS = 768


def expert_kernel(sizes, first_ref, *refs):
    groups, block_rows, capacity, step = sizes
    ins = refs[:groups]
    gate_up_ref, down_ref = refs[groups : groups + 2]
    tokens_ref, ring_ref, packed_ref, sum_ref, gate_ref, placer_ref, sem, token_sem = refs[-8:]
    outs = refs[-8 - groups : -8]
    experts, units, width = down_ref.shape
    tokens_n = ins[0].shape[0]
    per_group = tokens_n // block_rows
    span = per_group * capacity
    slots_n = experts * span

    columns = [slice(at, min(at + COLUMNS, width)) for at in range(0, width, COLUMNS)]

    pieces = [
        (expert, matrix, start, min(step, units - start))
        for expert in range(experts)
        for start in range(0, units, step)
        for matrix in range(3)
    ]

    def piece_copy(number):
        expert, matrix, start, rows = pieces[number]
        if matrix == 2:
            source = down_ref.at[expert, pl.ds(start, rows)]
        else:
            source = gate_up_ref.at[expert, matrix, pl.ds(start, rows)]
        slot = number % PIECE_SLOTS
        return pltpu.make_async_copy(source, ring_ref.at[slot, pl.ds(0, rows)], sem.at[slot])

    def use(wanted, product):
        number = pieces.index(wanted)
        piece_copy(number).wait()
        result = product(ring_ref.at[number % PIECE_SLOTS, pl.ds(0, wanted[3])])
        if number + PIECE_SLOTS < len(pieces):
            piece_copy(number + PIECE_SLOTS).start()
        return result

    def token_copy(group):
        return pltpu.make_async_copy(ins[group], tokens_ref.at[group], token_sem.at[group])

    def out_copy(group):
        return pltpu.make_async_copy(tokens_ref.at[group], outs[group], token_sem.at[group])

    for group in range(groups):
        token_copy(group).start()
    for number in range(min(PIECE_SLOTS, len(pieces))):
        piece_copy(number).start()

    slot = lax.broadcasted_iota(jnp.int32, (slots_n, tokens_n), 0)
    token = lax.broadcasted_iota(jnp.int32, (slots_n, tokens_n), 1)
    expert_of = (slot // span + first_ref[0]).astype(jnp.float32)
    place_of = (slot % capacity).astype(jnp.float32)
    own_block = (slot // capacity) % per_group == token // block_rows
    before = lax.broadcasted_iota(jnp.int32, (tokens_n, tokens_n), 0)
    after = lax.broadcasted_iota(jnp.int32, (tokens_n, tokens_n), 1)
    earlier = (before // block_rows == after // block_rows) & (before < after)
    earlier = jnp.where(earlier, 1.0, 0.0).astype(jnp.bfloat16)
    start = width + ROUTING - 128
    for group in range(groups):
        token_copy(group).wait()
        tail = tokens_ref[group, :, start : start + 128].astype(jnp.float32)
        tail = jnp.transpose(tail)[128 - ROUTING :]
        member = jnp.zeros((slots_n, tokens_n), jnp.float32)
        gate = jnp.zeros((slots_n, tokens_n), jnp.float32)
        for choice in range(TOPK):
            hit = tail[choice : choice + 1] == expert_of
            weight = (
                tail[TOPK + choice : TOPK + choice + 1]
                + tail[2 * TOPK + choice : 2 * TOPK + choice + 1]
                + tail[3 * TOPK + choice : 3 * TOPK + choice + 1]
            )
            member = member + jnp.where(hit, 1.0, 0.0)
            gate = gate + jnp.where(hit, weight, 0.0)
        rank = jnp.dot(member.astype(jnp.bfloat16), earlier, preferred_element_type=jnp.float32)
        chosen = own_block & (rank == place_of) & (member > 0.5)
        hot = jnp.where(chosen, 1.0, 0.0)
        gate = jnp.sum(jnp.where(chosen, gate, 0.0), axis=1, keepdims=True)
        placer_ref[group] = jnp.transpose(hot).astype(jnp.bfloat16)
        hot = hot.astype(jnp.bfloat16)
        for cut in columns:
            packed = jnp.dot(hot, tokens_ref[group, :, cut], preferred_element_type=jnp.float32)
            packed = packed.astype(jnp.bfloat16)
            for expert in range(experts):
                packed_ref[expert, group * span : (group + 1) * span, cut] = packed[
                    expert * span : (expert + 1) * span
                ]
        for expert in range(experts):
            place = slice(group * span, (group + 1) * span)
            gate_ref[expert, place] = jnp.broadcast_to(
                gate[expert * span : (expert + 1) * span], (span, 128)
            )

    for expert in range(experts):
        rows = packed_ref[expert]

        def project(weight):
            return lax.dot_general(
                rows, weight, (((1,), (1,)), ((), ())), preferred_element_type=jnp.float32
            )

        for start in range(0, units, step):
            length = min(step, units - start)
            gate = use((expert, 0, start, length), lambda ref: project(ref[...]))
            up = use((expert, 1, start, length), lambda ref: project(ref[...]))
            act = gate / (1.0 + jnp.exp(-gate)) * up * gate_ref[expert][:, :1]
            act = act.astype(jnp.bfloat16)

            def add(weight_ref):
                for cut in columns:
                    part = jnp.dot(act, weight_ref[:, cut], preferred_element_type=jnp.float32)
                    sum_ref[:, cut] = sum_ref[:, cut] + part if start else part

            use((expert, 2, start, length), add)
        for cut in columns:
            packed_ref[expert, :, cut] = sum_ref[:, cut].astype(jnp.bfloat16)

    for group in range(groups):
        place = slice(group * span, (group + 1) * span)
        for cut in columns:
            rows = [packed_ref[expert, place, cut] for expert in range(experts)]
            rows = jnp.concatenate(rows, axis=0)
            summed = jnp.dot(placer_ref[group], rows, preferred_element_type=jnp.float32)
            tokens_ref[group, :, cut] = summed.astype(jnp.bfloat16)
        out_copy(group).start()
    for group in range(groups):
        out_copy(group).wait()


def run_experts(first, tokens, gate_up, down, block_rows, capacity):
    groups = len(tokens)
    tokens_n, wide = tokens[0].shape
    experts, units, width = down.shape
    span = tokens_n // block_rows * capacity
    slots_n = experts * span
    step = units if units % 16 else PIECE_ROWS
    padded = -(-width // 128) * 128
    scratch = 2 * padded * (groups * tokens_n + PIECE_SLOTS * min(step, units))
    scratch += 2 * padded * (experts + 2) * groups * span + 512 * experts * groups * span
    scratch += 2 * groups * tokens_n * slots_n
    anywhere = pl.BlockSpec(memory_space=pl.ANY)
    return pl.pallas_call(
        functools.partial(expert_kernel, (groups, block_rows, capacity, step)),
        in_specs=[pl.BlockSpec(memory_space=pltpu.SMEM)]
        + [anywhere] * (groups + 2),
        out_specs=[anywhere] * groups,
        out_shape=[jax.ShapeDtypeStruct((tokens_n, wide), jnp.bfloat16)] * groups,
        scratch_shapes=[
            pltpu.VMEM((groups, tokens_n, wide), jnp.bfloat16),
            pltpu.VMEM((PIECE_SLOTS, min(step, units), width), jnp.bfloat16),
            pltpu.VMEM((experts, groups * span, width), jnp.bfloat16),
            pltpu.VMEM((groups * span, width), jnp.float32),
            pltpu.VMEM((experts, groups * span, 128), jnp.float32),
            pltpu.VMEM((groups, tokens_n, slots_n), jnp.bfloat16),
            pltpu.SemaphoreType.DMA((PIECE_SLOTS,)),
            pltpu.SemaphoreType.DMA((groups,)),
        ],
        compiler_params=pltpu.CompilerParams(vmem_limit_bytes=scratch + EXPERT_KERNEL),
        cost_estimate=pl.CostEstimate(
            flops=6 * slots_n * groups * width * units,
            bytes_accessed=6 * experts * width * units,
            transcendentals=0,
        ),
    )(first, *tokens, gate_up, down)


def rms_scale(values, gain_vec):
    mean_sq = jnp.mean(values * values, axis=-1, keepdims=True)
    return values * lax.rsqrt(mean_sq + EPS) * gain_vec


def window_block(queries, key_rows, value_rows):
    scores = jnp.einsum(
        "qhgc,khc->hgqk", queries, key_rows, preferred_element_type=jnp.float32
    ) * HEAD_SIZE ** (-0.5)
    key_offset = jnp.arange(key_rows.shape[0])[None, :] - jnp.arange(queries.shape[0])[:, None]
    in_window = (key_offset >= 1) & (key_offset <= WINDOW_KEYS)
    scores = jnp.where(in_window, scores, -1e30)
    row_max = jnp.max(scores, axis=-1, keepdims=True)
    exponent = jnp.exp(scores - row_max)
    layer_weights = (exponent / jnp.sum(exponent, axis=-1, keepdims=True)).astype(jnp.bfloat16)
    attended = jnp.einsum(
        "hgqk,khc->qhgc", layer_weights, value_rows, preferred_element_type=jnp.float32
    )
    return attended.astype(jnp.bfloat16)


def local(
    stream_in,
    attn_gain,
    w_qkv,
    key_value_cache,
    w_out,
    mlp_gain,
    expert_index,
    gate_weight,
    w_gateup,
    w_down,
):
    seq_count = lax.axis_size("seq")
    tp_count = lax.axis_size("tp")
    length_local = stream_in.shape[0]
    heads_local = w_qkv.shape[1]
    query_group_width = QUERY_HEADS // KEY_VALUE_HEADS
    normed = rms_scale(stream_in.astype(jnp.float32), attn_gain).astype(jnp.bfloat16)
    projected_rows = jnp.einsum(
        "td,dhc->thc", normed, w_qkv, preferred_element_type=jnp.float32
    ).astype(jnp.bfloat16)
    projected_rows = projected_rows.reshape(
        length_local, heads_local, query_group_width + 2, HEAD_SIZE
    )
    queries = projected_rows[:, :, :query_group_width]
    kv_tail_rows = jnp.concatenate(
        [
            projected_rows[length_local - WINDOW_KEYS :, :, query_group_width],
            projected_rows[length_local - WINDOW_KEYS :, :, query_group_width + 1],
        ],
        axis=-1,
    )
    earlier = from_behind(kv_tail_rows, "seq", 1)
    at_start = lax.axis_index("seq") == 0
    earlier = jnp.where(at_start, key_value_cache, earlier)
    key_rows = jnp.concatenate(
        [earlier[:, :, :HEAD_SIZE], projected_rows[:, :, query_group_width]], axis=0
    )
    value_rows = jnp.concatenate(
        [earlier[:, :, HEAD_SIZE:], projected_rows[:, :, query_group_width + 1]], axis=0
    )
    attended = window_block(queries, key_rows, value_rows).reshape(
        length_local, heads_local * query_group_width * HEAD_SIZE
    )
    block_rows = length_local // tp_count
    plan = axis_plan(seq_count, tp_count)
    across = tp_count // 2

    terms = jnp.dot(attended, w_out, preferred_element_type=jnp.float32)
    terms = terms.reshape(across, 2, block_rows, MODEL_WIDTH)
    core = lax.axis_index("tp") % 2
    kept = lax.dynamic_index_in_dim(terms, core, 1, False)
    handed = lax.dynamic_index_in_dim(terms, 1 - core, 1, False).astype(jnp.bfloat16)
    kept = kept + swap(handed, 1, 1).astype(jnp.float32)
    place = lax.axis_index("tp") // 2
    attn_out = lax.dynamic_index_in_dim(kept, place, 0, False)
    for other in range(1, across):
        handed_on = lax.dynamic_index_in_dim(kept, place ^ other, 0, False).astype(jnp.bfloat16)
        attn_out = attn_out + swap(handed_on, 2 * other, 2 * other).astype(jnp.float32)
    own_start = lax.axis_index("tp") * block_rows
    residual = (
        lax.dynamic_slice_in_dim(stream_in, own_start, block_rows, 0).astype(jnp.float32) + attn_out
    )
    hidden_in = rms_scale(residual, mlp_gain).astype(jnp.bfloat16)

    experts_dev = w_gateup.shape[0]
    capacity = 2 * length_local * TOPK // (tp_count * EXPERTS)
    high = lax.reduce_precision(gate_weight, 8, 7)
    middle = lax.reduce_precision(gate_weight - high, 8, 7)
    low = lax.reduce_precision(gate_weight - high - middle, 8, 7)
    routing = jnp.concatenate([expert_index.astype(jnp.float32), high, middle, low], axis=1)
    routing = jnp.pad(routing, ((0, 0), (0, ROUTING - 4 * TOPK))).astype(jnp.bfloat16)
    gate_up = jnp.transpose(w_gateup, (0, 2, 3, 1))
    gate_up = pltpu.with_memory_space_constraint(gate_up, pltpu.HBM)
    down = pltpu.with_memory_space_constraint(w_down, pltpu.HBM)
    rows = jnp.concatenate([hidden_in, routing], axis=1)

    (slow, slow_step, _), inner = plan[0], plan[1:]
    (size, even, odd), (last_size, last_even, last_odd) = inner
    half = slow // 2

    def along(value, offset):
        return swap(value, offset * slow_step, offset * slow_step)

    even_pieces = [along(rows, offset) for offset in range(2, slow, 2)]
    odd_pieces = [along(rows, 1)]
    odd_pieces += [along(join([rows], 1, even_pieces), offset) for offset in range(3, slow, 2)]
    spread_own = spread(rows, inner)
    even_pieces = [join([piece], 1, [spread_own[1], spread_own[size]]) for piece in even_pieces]
    pieces_a = spread_own + [piece for start in even_pieces for piece in spread(start, inner)]
    pair = join(odd_pieces, 1, pieces_a[-size * last_size + 1 :][: size])
    mine_a = join(pieces_a)
    theirs_a = swap(mine_a, 1, 1)
    pieces_b = spread(pair, inner)
    mine_b = join(pieces_b, half)
    tokens = [mine_a, theirs_a, mine_b, swap(mine_b, 1, 1)]

    first = (lax.axis_index("seq") * experts_dev).astype(jnp.int32).reshape(1)
    sums = run_experts(first, tokens, gate_up, down, block_rows, capacity)

    kinds = ([jnp.float32] + [jnp.bfloat16] * (last_size - 1)) * half
    inner_kinds = [jnp.float32] + [jnp.bfloat16] * (size - 1)
    parts = [fold([kept, swap(handed, 1, 1)], kinds) for kept, handed in (sums[:2], sums[2:])]
    arrived = []
    after = []
    for offset in list(range(slow - 1, 1, -1)) + [1, 0]:
        place = offset // 2 * last_size
        terms = send_parts(parts[offset % 2][place : place + last_size], last_even, last_odd)
        terms = send_parts(fold(terms, inner_kinds, after + arrived[-2:-1]), even, odd)
        if offset:
            after = list(fold(terms, [jnp.bfloat16]))
            arrived.append(along(after[0], offset))
        else:
            total = residual + fold(terms, [jnp.float32])[0][:, :MODEL_WIDTH]
    for part in arrived:
        total = total + part[:, :MODEL_WIDTH].astype(jnp.float32)
    return total.astype(jnp.bfloat16)


def solution(mesh):
    in_specs = (
        P("seq", None),
        P(),
        P(None, "tp", None),
        P(None, "tp", None),
        P("tp", None),
        P(),
        P(("seq", "tp"), None),
        P(("seq", "tp"), None),
        P("seq", None, None, "tp"),
        P("seq", "tp", None),
    )
    out_specs = P(("seq", "tp"), None)
    return jax.shard_map(local, mesh=mesh, in_specs=in_specs, out_specs=out_specs, check_vma=False)
```

```python
import functools

import jax
import jax.numpy as jnp
from jax import lax
from jax.experimental import pallas as pl
from jax.experimental.pallas import tpu as pltpu
from jax.sharding import PartitionSpec as P

MODEL_WIDTH = 2880
QUERY_HEADS = 64
KEY_VALUE_HEADS = 8
HEAD_SIZE = 64
WINDOW_KEYS = 128
EXPERTS = 32
TOPK = 4


EPS = 1e-05


def from_behind(value, axis, steps):
    count = lax.axis_size(axis)
    first, last = (max(0, -steps), min(count, count - steps))
    return lax.ppermute(value, axis, [(source, source + steps) for source in range(first, last)])


def axis_plan(seq_count, tp_count):
    across = tp_count // 2
    slow = min(4, seq_count)
    quick = seq_count // slow
    x_step, quick_step, slow_step = 2, 2 * across, 2 * across * quick
    along = [(slow, slow_step, slow_step)]
    if across == quick:
        along.append((across, x_step, quick_step))
        along.append((across, quick_step, x_step))
    else:
        along.append((across, x_step, x_step))
        along.append((quick, quick_step, quick_step))
    return along


def swap(value, even_mask, odd_mask):
    count = lax.axis_size("seq") * lax.axis_size("tp")
    pairs = [
        (device, device ^ (odd_mask if device % 2 else even_mask)) for device in range(count)
    ]
    return lax.ppermute(value, ("seq", "tp"), pairs)


def spread(piece, steps):
    pieces = [piece]
    for size, even, odd in steps:
        pieces = pieces + [
            swap(held, other * even, other * odd) for other in range(1, size) for held in pieces
        ]
    return pieces


ROUTING = 64
SMALL_KERNEL = 8 << 20


def join_kernel(count, pieces, *refs):
    parts, out_ref = refs[:count], refs[-1]
    rows = parts[0].shape[0] // pieces
    for piece in range(pieces):
        for place, part in enumerate(parts):
            start = (piece * count + place) * rows
            out_ref[start : start + rows, :] = part[piece * rows : (piece + 1) * rows, :]


def join(parts, pieces=1, after=()):
    rows, width = parts[0].shape
    return pl.pallas_call(
        functools.partial(join_kernel, len(parts), pieces),
        in_specs=[pl.BlockSpec(memory_space=pltpu.VMEM)] * len(parts)
        + [pl.BlockSpec(memory_space=pl.ANY)] * len(after),
        out_shape=jax.ShapeDtypeStruct((len(parts) * rows, width), parts[0].dtype),
        compiler_params=pltpu.CompilerParams(vmem_limit_bytes=SMALL_KERNEL),
        cost_estimate=pl.CostEstimate(
            flops=0, bytes_accessed=4 * len(parts) * rows * width, transcendentals=0
        ),
    )(*parts, *after)


def fold_kernel(count, outs_n, *refs):
    terms, outs = refs[:count], refs[len(refs) - outs_n :]
    rows = outs[0].shape[0]
    for place, out_ref in enumerate(outs):
        cut = slice(place * rows, (place + 1) * rows)
        total = terms[0][cut, :].astype(jnp.float32)
        for term in terms[1:]:
            total = total + term[cut, :].astype(jnp.float32)
        out_ref[...] = total.astype(out_ref.dtype)


def fold(terms, kinds, after=()):
    rows, width = terms[0].shape
    rows = rows // len(kinds)
    return pl.pallas_call(
        functools.partial(fold_kernel, len(terms), len(kinds)),
        in_specs=[pl.BlockSpec(memory_space=pltpu.VMEM)] * len(terms)
        + [pl.BlockSpec(memory_space=pl.ANY)] * len(after),
        out_shape=[jax.ShapeDtypeStruct((rows, width), kind) for kind in kinds],
        compiler_params=pltpu.CompilerParams(vmem_limit_bytes=SMALL_KERNEL),
        cost_estimate=pl.CostEstimate(
            flops=len(terms) * rows * len(kinds) * width,
            bytes_accessed=4 * len(terms) * rows * len(kinds) * width,
            transcendentals=0,
        ),
    )(*terms, *after)


def send_parts(parts, even, odd):
    return [parts[0]] + [
        swap(part, other * even, other * odd) for other, part in enumerate(parts[1:], 1)
    ]


def expert_kernel(sizes, first_ref, *refs):
    groups, block_rows, capacity = sizes
    ins = refs[:groups]
    gate_up_ref, down_ref = refs[groups : groups + 2]
    outs = refs[groups + 2 : 2 * groups + 2]
    tokens_ref, gate_up_buf, down_buf, packed_ref, gate_ref, placer_ref = refs[2 * groups + 2 : -4]
    token_sem, gate_up_sem, down_sem, out_sem = refs[-4:]
    experts, _, units, width = gate_up_ref.shape
    tokens_n = ins[0].shape[0]
    per_group = tokens_n // block_rows
    span = per_group * capacity
    slots_n = experts * span

    def token_copy(group):
        return pltpu.make_async_copy(ins[group], tokens_ref.at[group], token_sem.at[group])

    def out_copy(group):
        return pltpu.make_async_copy(tokens_ref.at[group], outs[group], out_sem.at[group])

    def gate_up_copy(expert):
        return pltpu.make_async_copy(
            gate_up_ref.at[expert], gate_up_buf.at[expert % 2], gate_up_sem.at[expert % 2]
        )

    def down_copy(expert):
        return pltpu.make_async_copy(
            down_ref.at[expert], down_buf.at[expert % 2], down_sem.at[expert % 2]
        )

    for group in range(groups):
        token_copy(group).start()
    gate_up_copy(0).start()
    down_copy(0).start()

    slot = lax.broadcasted_iota(jnp.int32, (slots_n, tokens_n), 0)
    token = lax.broadcasted_iota(jnp.int32, (slots_n, tokens_n), 1)
    expert_of = (slot // span + first_ref[0]).astype(jnp.float32)
    place_of = (slot % capacity).astype(jnp.float32)
    own_block = (slot // capacity) % per_group == token // block_rows
    before = lax.broadcasted_iota(jnp.int32, (tokens_n, tokens_n), 0)
    after = lax.broadcasted_iota(jnp.int32, (tokens_n, tokens_n), 1)
    earlier = (before // block_rows == after // block_rows) & (before < after)
    earlier = jnp.where(earlier, 1.0, 0.0).astype(jnp.bfloat16)
    start = width + ROUTING - 128
    for group in range(groups):
        token_copy(group).wait()
        tail = tokens_ref[group, :, start : start + 128].astype(jnp.float32)
        tail = jnp.transpose(tail)[128 - ROUTING :]
        member = jnp.zeros((slots_n, tokens_n), jnp.float32)
        gate = jnp.zeros((slots_n, tokens_n), jnp.float32)
        for choice in range(TOPK):
            hit = tail[choice : choice + 1] == expert_of
            weight = (
                tail[TOPK + choice : TOPK + choice + 1]
                + tail[2 * TOPK + choice : 2 * TOPK + choice + 1]
                + tail[3 * TOPK + choice : 3 * TOPK + choice + 1]
            )
            member = member + jnp.where(hit, 1.0, 0.0)
            gate = gate + jnp.where(hit, weight, 0.0)
        rank = jnp.dot(member.astype(jnp.bfloat16), earlier, preferred_element_type=jnp.float32)
        chosen = own_block & (rank == place_of) & (member > 0.5)
        hot = jnp.where(chosen, 1.0, 0.0)
        gate = jnp.sum(jnp.where(chosen, gate, 0.0), axis=1, keepdims=True)
        placer_ref[group] = jnp.transpose(hot).astype(jnp.bfloat16)
        rows = tokens_ref[group, :, :width]
        packed = jnp.dot(hot.astype(jnp.bfloat16), rows, preferred_element_type=jnp.float32)
        packed = packed.astype(jnp.bfloat16)
        for expert in range(experts):
            place = slice(group * span, (group + 1) * span)
            packed_ref[expert, place] = packed[expert * span : (expert + 1) * span]
            gate_ref[expert, place] = jnp.broadcast_to(
                gate[expert * span : (expert + 1) * span], (span, 128)
            )

    contract = (((1,), (1,)), ((), ()))
    for expert in range(experts):
        held = expert % 2
        if expert + 1 < experts:
            gate_up_copy(expert + 1).start()
            down_copy(expert + 1).start()
        gate_up_copy(expert).wait()
        rows = packed_ref[expert]
        both = lax.dot_general(
            rows,
            gate_up_buf[held].reshape(2 * units, width),
            contract,
            preferred_element_type=jnp.float32,
        )
        gate, up = both[:, :units], both[:, units:]
        act = gate / (1.0 + jnp.exp(-gate)) * up * gate_ref[expert][:, :1]
        act = act.astype(jnp.bfloat16)
        down_copy(expert).wait()
        result = jnp.dot(act, down_buf[held], preferred_element_type=jnp.float32)
        packed_ref[expert] = result.astype(jnp.bfloat16)

    for group in range(groups):
        place = slice(group * span, (group + 1) * span)
        rows = jnp.concatenate([packed_ref[expert, place] for expert in range(experts)], axis=0)
        summed = jnp.dot(placer_ref[group], rows, preferred_element_type=jnp.float32)
        tokens_ref[group, :, :width] = summed.astype(jnp.bfloat16)
        out_copy(group).start()
    for group in range(groups):
        out_copy(group).wait()


def run_experts(first, tokens, gate_up, down, block_rows, capacity):
    groups = len(tokens)
    tokens_n, wide = tokens[0].shape
    experts, _, units, width = gate_up.shape
    span = tokens_n // block_rows * capacity
    slots_n = experts * span
    anywhere = pl.BlockSpec(memory_space=pl.ANY)
    return pl.pallas_call(
        functools.partial(expert_kernel, (groups, block_rows, capacity)),
        in_specs=[pl.BlockSpec(memory_space=pltpu.SMEM)] + [anywhere] * (groups + 2),
        out_specs=[anywhere] * groups,
        out_shape=[jax.ShapeDtypeStruct((tokens_n, wide), jnp.bfloat16)] * groups,
        scratch_shapes=[
            pltpu.VMEM((groups, tokens_n, wide), jnp.bfloat16),
            pltpu.VMEM((2, 2, units, width), jnp.bfloat16),
            pltpu.VMEM((2, units, width), jnp.bfloat16),
            pltpu.VMEM((experts, groups * span, width), jnp.bfloat16),
            pltpu.VMEM((experts, groups * span, 128), jnp.float32),
            pltpu.VMEM((groups, tokens_n, slots_n), jnp.bfloat16),
            pltpu.SemaphoreType.DMA((groups,)),
            pltpu.SemaphoreType.DMA((2,)),
            pltpu.SemaphoreType.DMA((2,)),
            pltpu.SemaphoreType.DMA((groups,)),
        ],
        compiler_params=pltpu.CompilerParams(vmem_limit_bytes=52 << 20),
        cost_estimate=pl.CostEstimate(
            flops=6 * slots_n * groups * width * units,
            bytes_accessed=6 * experts * width * units,
            transcendentals=0,
        ),
    )(first, *tokens, gate_up, down)


def rms_scale(values, gain_vec):
    mean_sq = jnp.mean(values * values, axis=-1, keepdims=True)
    return values * lax.rsqrt(mean_sq + EPS) * gain_vec


def window_block(queries, key_rows, value_rows):
    scores = jnp.einsum(
        "qhgc,khc->hgqk", queries, key_rows, preferred_element_type=jnp.float32
    ) * HEAD_SIZE ** (-0.5)
    key_offset = jnp.arange(key_rows.shape[0])[None, :] - jnp.arange(queries.shape[0])[:, None]
    in_window = (key_offset >= 1) & (key_offset <= WINDOW_KEYS)
    scores = jnp.where(in_window, scores, -1e30)
    row_max = jnp.max(scores, axis=-1, keepdims=True)
    exponent = jnp.exp(scores - row_max)
    layer_weights = (exponent / jnp.sum(exponent, axis=-1, keepdims=True)).astype(jnp.bfloat16)
    attended = jnp.einsum(
        "hgqk,khc->qhgc", layer_weights, value_rows, preferred_element_type=jnp.float32
    )
    return attended.astype(jnp.bfloat16)


def local(
    stream_in,
    attn_gain,
    w_qkv,
    key_value_cache,
    w_out,
    mlp_gain,
    expert_index,
    gate_weight,
    w_gateup,
    w_down,
):
    seq_count = lax.axis_size("seq")
    tp_count = lax.axis_size("tp")
    length_local = stream_in.shape[0]
    heads_local = w_qkv.shape[1]
    query_group_width = QUERY_HEADS // KEY_VALUE_HEADS
    normed = rms_scale(stream_in.astype(jnp.float32), attn_gain).astype(jnp.bfloat16)
    projected_rows = jnp.einsum(
        "td,dhc->thc", normed, w_qkv, preferred_element_type=jnp.float32
    ).astype(jnp.bfloat16)
    projected_rows = projected_rows.reshape(
        length_local, heads_local, query_group_width + 2, HEAD_SIZE
    )
    queries = projected_rows[:, :, :query_group_width]
    kv_tail_rows = jnp.concatenate(
        [
            projected_rows[length_local - WINDOW_KEYS :, :, query_group_width],
            projected_rows[length_local - WINDOW_KEYS :, :, query_group_width + 1],
        ],
        axis=-1,
    )
    earlier = from_behind(kv_tail_rows, "seq", 1)
    at_start = lax.axis_index("seq") == 0
    earlier = jnp.where(at_start, key_value_cache, earlier)
    key_rows = jnp.concatenate(
        [earlier[:, :, :HEAD_SIZE], projected_rows[:, :, query_group_width]], axis=0
    )
    value_rows = jnp.concatenate(
        [earlier[:, :, HEAD_SIZE:], projected_rows[:, :, query_group_width + 1]], axis=0
    )
    attended = window_block(queries, key_rows, value_rows).reshape(
        length_local, heads_local * query_group_width * HEAD_SIZE
    )
    block_rows = length_local // tp_count
    plan = axis_plan(seq_count, tp_count)
    across = tp_count // 2

    terms = jnp.dot(attended, w_out, preferred_element_type=jnp.float32)
    terms = terms.reshape(across, 2, block_rows, MODEL_WIDTH)
    core = lax.axis_index("tp") % 2
    kept = lax.dynamic_index_in_dim(terms, core, 1, False)
    handed = lax.dynamic_index_in_dim(terms, 1 - core, 1, False).astype(jnp.bfloat16)
    kept = kept + swap(handed, 1, 1).astype(jnp.float32)
    place = lax.axis_index("tp") // 2
    attn_out = lax.dynamic_index_in_dim(kept, place, 0, False)
    for other in range(1, across):
        handed_on = lax.dynamic_index_in_dim(kept, place ^ other, 0, False).astype(jnp.bfloat16)
        attn_out = attn_out + swap(handed_on, 2 * other, 2 * other).astype(jnp.float32)
    own_start = lax.axis_index("tp") * block_rows
    residual = (
        lax.dynamic_slice_in_dim(stream_in, own_start, block_rows, 0).astype(jnp.float32) + attn_out
    )
    hidden_in = rms_scale(residual, mlp_gain).astype(jnp.bfloat16)

    experts_dev = w_gateup.shape[0]
    capacity = 2 * length_local * TOPK // (tp_count * EXPERTS)
    high = lax.reduce_precision(gate_weight, 8, 7)
    middle = lax.reduce_precision(gate_weight - high, 8, 7)
    low = lax.reduce_precision(gate_weight - high - middle, 8, 7)
    routing = jnp.concatenate([expert_index.astype(jnp.float32), high, middle, low], axis=1)
    routing = jnp.pad(routing, ((0, 0), (0, ROUTING - 4 * TOPK))).astype(jnp.bfloat16)
    gate_up = jnp.transpose(w_gateup, (0, 2, 3, 1))
    gate_up = pltpu.with_memory_space_constraint(gate_up, pltpu.HBM)
    down = pltpu.with_memory_space_constraint(w_down, pltpu.HBM)
    rows = jnp.concatenate([hidden_in, routing], axis=1)

    (slow, slow_step, _), inner = plan[0], plan[1:]
    (size, even, odd), (last_size, last_even, last_odd) = inner
    half = slow // 2

    def along(value, offset):
        return swap(value, offset * slow_step, offset * slow_step)

    others = [along(rows, offset) for offset in range(1, slow)]
    first_pieces, second_pieces = [rows] + others[: half - 1], others[half - 1 :]
    spread_a = [spread(rows, inner)]
    for piece in first_pieces[1:]:
        spread_a.append(spread(join([piece], 1, spread_a[0][1:2]), inner))
    forwards = [piece for pieces in spread_a for piece in pieces[1 : size + 1]]
    pieces_b = spread(join(second_pieces, 1, forwards + spread_a[0][size + 1 :]), inner)
    mine_a = join([piece for pieces in spread_a for piece in pieces])
    mine_b = join(pieces_b, half)
    tokens = [mine_a, swap(mine_a, 1, 1), mine_b, swap(mine_b, 1, 1)]

    first = (lax.axis_index("seq") * experts_dev).astype(jnp.int32).reshape(1)
    sums = run_experts(first, tokens, gate_up, down, block_rows, capacity)

    kinds = ([jnp.float32] + [jnp.bfloat16] * (last_size - 1)) * half
    inner_kinds = [jnp.float32] + [jnp.bfloat16] * (size - 1)
    parts = [fold([kept, swap(handed, 1, 1)], kinds) for kept, handed in (sums[:2], sums[2:])]
    arrived = []
    after = []
    for offset in list(range(slow - 1, 1, -1)) + [1, 0]:
        place = offset % half * last_size
        terms = send_parts(parts[offset // half][place : place + last_size], last_even, last_odd)
        terms = send_parts(fold(terms, inner_kinds, after + arrived[-2:-1]), even, odd)
        if offset:
            after = list(fold(terms, [jnp.bfloat16]))
            arrived.append(along(after[0], offset))
        else:
            total = residual + fold(terms, [jnp.float32], arrived[-1:])[0][:, :MODEL_WIDTH]
    for part in arrived:
        total = total + part[:, :MODEL_WIDTH].astype(jnp.float32)
    return total.astype(jnp.bfloat16)


def solution(mesh):
    in_specs = (
        P("seq", None),
        P(),
        P(None, "tp", None),
        P(None, "tp", None),
        P("tp", None),
        P(),
        P(("seq", "tp"), None),
        P(("seq", "tp"), None),
        P("seq", None, None, "tp"),
        P("seq", "tp", None),
    )
    out_specs = P(("seq", "tp"), None)
    return jax.shard_map(local, mesh=mesh, in_specs=in_specs, out_specs=out_specs, check_vma=False)
```

```python
import functools

import jax
import jax.numpy as jnp
from jax import lax
from jax.experimental import pallas as pl
from jax.experimental.pallas import tpu as pltpu
from jax.sharding import PartitionSpec as P

MODEL_WIDTH = 2880
QUERY_HEADS = 64
KEY_VALUE_HEADS = 8
HEAD_SIZE = 64
WINDOW_KEYS = 128
EXPERTS = 32
TOPK = 4


EPS = 1e-05


def from_behind(value, axis, steps):
    count = lax.axis_size(axis)
    first, last = (max(0, -steps), min(count, count - steps))
    return lax.ppermute(value, axis, [(source, source + steps) for source in range(first, last)])


def axis_plan(seq_count, tp_count):
    across = tp_count // 2
    slow = min(4, seq_count)
    quick = seq_count // slow
    x_step, quick_step, slow_step = 2, 2 * across, 2 * across * quick
    along = [(slow, slow_step, slow_step)]
    if across == quick:
        along.append((across, x_step, quick_step))
        along.append((across, quick_step, x_step))
    else:
        along.append((across, x_step, x_step))
        along.append((quick, quick_step, quick_step))
    return along


def swap(value, even_mask, odd_mask):
    count = lax.axis_size("seq") * lax.axis_size("tp")
    pairs = [
        (device, device ^ (odd_mask if device % 2 else even_mask)) for device in range(count)
    ]
    return lax.ppermute(value, ("seq", "tp"), pairs)


def spread(piece, steps):
    pieces = [piece]
    for size, even, odd in steps:
        pieces = pieces + [
            swap(held, other * even, other * odd) for other in range(1, size) for held in pieces
        ]
    return pieces


ROUTING = 64
SMALL_KERNEL = 8 << 20


def join_kernel(count, pieces, *refs):
    parts, out_ref = refs[:count], refs[-1]
    rows = parts[0].shape[0] // pieces
    for piece in range(pieces):
        for place, part in enumerate(parts):
            start = (piece * count + place) * rows
            out_ref[start : start + rows, :] = part[piece * rows : (piece + 1) * rows, :]


def join(parts, pieces=1, after=()):
    rows, width = parts[0].shape
    return pl.pallas_call(
        functools.partial(join_kernel, len(parts), pieces),
        in_specs=[pl.BlockSpec(memory_space=pltpu.VMEM)] * len(parts)
        + [pl.BlockSpec(memory_space=pl.ANY)] * len(after),
        out_shape=jax.ShapeDtypeStruct((len(parts) * rows, width), parts[0].dtype),
        compiler_params=pltpu.CompilerParams(vmem_limit_bytes=SMALL_KERNEL),
        cost_estimate=pl.CostEstimate(
            flops=0, bytes_accessed=4 * len(parts) * rows * width, transcendentals=0
        ),
    )(*parts, *after)


def fold_kernel(count, outs_n, first_row, *refs):
    terms, outs = refs[:count], refs[len(refs) - outs_n :]
    rows = outs[0].shape[0]
    for place, out_ref in enumerate(outs):
        cut = slice(first_row + place * rows, first_row + (place + 1) * rows)
        total = terms[0][cut, :].astype(jnp.float32)
        for term in terms[1:]:
            total = total + term[cut, :].astype(jnp.float32)
        out_ref[...] = total.astype(out_ref.dtype)


def fold(terms, kinds, after=(), piece=0, pieces=1):
    rows, width = terms[0].shape
    rows = rows // (pieces * len(kinds))
    return pl.pallas_call(
        functools.partial(fold_kernel, len(terms), len(kinds), piece * len(kinds) * rows),
        in_specs=[pl.BlockSpec(memory_space=pltpu.VMEM)] * len(terms)
        + [pl.BlockSpec(memory_space=pl.ANY)] * len(after),
        out_shape=[jax.ShapeDtypeStruct((rows, width), kind) for kind in kinds],
        compiler_params=pltpu.CompilerParams(vmem_limit_bytes=SMALL_KERNEL),
        cost_estimate=pl.CostEstimate(
            flops=len(terms) * rows * len(kinds) * width,
            bytes_accessed=4 * len(terms) * rows * len(kinds) * width,
            transcendentals=0,
        ),
    )(*terms, *after)


def send_parts(parts, even, odd):
    return [parts[0]] + [
        swap(part, other * even, other * odd) for other, part in enumerate(parts[1:], 1)
    ]


def expert_kernel(sizes, first_ref, *refs):
    groups, block_rows, capacity = sizes
    ins = refs[:groups]
    gate_up_ref, down_ref = refs[groups : groups + 2]
    outs = refs[groups + 2 : 2 * groups + 2]
    tokens_ref, gate_up_buf, down_buf, packed_ref, gate_ref, placer_ref = refs[2 * groups + 2 : -4]
    token_sem, gate_up_sem, down_sem, out_sem = refs[-4:]
    experts, _, units, width = gate_up_ref.shape
    tokens_n = ins[0].shape[0]
    per_group = tokens_n // block_rows
    span = per_group * capacity
    slots_n = experts * span

    def token_copy(group):
        return pltpu.make_async_copy(ins[group], tokens_ref.at[group], token_sem.at[group])

    def out_copy(group):
        return pltpu.make_async_copy(tokens_ref.at[group], outs[group], out_sem.at[group])

    def gate_up_copy(expert):
        return pltpu.make_async_copy(
            gate_up_ref.at[expert], gate_up_buf.at[expert % 2], gate_up_sem.at[expert % 2]
        )

    def down_copy(expert):
        return pltpu.make_async_copy(
            down_ref.at[expert], down_buf.at[expert % 2], down_sem.at[expert % 2]
        )

    for group in range(groups):
        token_copy(group).start()
    gate_up_copy(0).start()
    down_copy(0).start()

    slot = lax.broadcasted_iota(jnp.int32, (slots_n, tokens_n), 0)
    token = lax.broadcasted_iota(jnp.int32, (slots_n, tokens_n), 1)
    expert_of = (slot // span + first_ref[0]).astype(jnp.float32)
    place_of = (slot % capacity).astype(jnp.float32)
    own_block = (slot // capacity) % per_group == token // block_rows
    before = lax.broadcasted_iota(jnp.int32, (tokens_n, tokens_n), 0)
    after = lax.broadcasted_iota(jnp.int32, (tokens_n, tokens_n), 1)
    earlier = (before // block_rows == after // block_rows) & (before < after)
    earlier = jnp.where(earlier, 1.0, 0.0).astype(jnp.bfloat16)
    start = width + ROUTING - 128
    for group in range(groups):
        token_copy(group).wait()
        tail = tokens_ref[group, :, start : start + 128].astype(jnp.float32)
        tail = jnp.transpose(tail)[128 - ROUTING :]
        member = jnp.zeros((slots_n, tokens_n), jnp.float32)
        gate = jnp.zeros((slots_n, tokens_n), jnp.float32)
        for choice in range(TOPK):
            hit = tail[choice : choice + 1] == expert_of
            weight = (
                tail[TOPK + choice : TOPK + choice + 1]
                + tail[2 * TOPK + choice : 2 * TOPK + choice + 1]
                + tail[3 * TOPK + choice : 3 * TOPK + choice + 1]
            )
            member = member + jnp.where(hit, 1.0, 0.0)
            gate = gate + jnp.where(hit, weight, 0.0)
        rank = jnp.dot(member.astype(jnp.bfloat16), earlier, preferred_element_type=jnp.float32)
        chosen = own_block & (rank == place_of) & (member > 0.5)
        hot = jnp.where(chosen, 1.0, 0.0)
        gate = jnp.sum(jnp.where(chosen, gate, 0.0), axis=1, keepdims=True)
        placer_ref[group] = jnp.transpose(hot).astype(jnp.bfloat16)
        rows = tokens_ref[group, :, :width]
        packed = jnp.dot(hot.astype(jnp.bfloat16), rows, preferred_element_type=jnp.float32)
        packed = packed.astype(jnp.bfloat16)
        for expert in range(experts):
            place = slice(group * span, (group + 1) * span)
            packed_ref[expert, place] = packed[expert * span : (expert + 1) * span]
            gate_ref[expert, place] = jnp.broadcast_to(
                gate[expert * span : (expert + 1) * span], (span, 128)
            )

    contract = (((1,), (1,)), ((), ()))
    for expert in range(experts):
        held = expert % 2
        if expert + 1 < experts:
            gate_up_copy(expert + 1).start()
            down_copy(expert + 1).start()
        gate_up_copy(expert).wait()
        rows = packed_ref[expert]
        both = lax.dot_general(
            rows,
            gate_up_buf[held].reshape(2 * units, width),
            contract,
            preferred_element_type=jnp.float32,
        )
        gate, up = both[:, :units], both[:, units:]
        act = gate / (1.0 + jnp.exp(-gate)) * up * gate_ref[expert][:, :1]
        act = act.astype(jnp.bfloat16)
        down_copy(expert).wait()
        result = jnp.dot(act, down_buf[held], preferred_element_type=jnp.float32)
        packed_ref[expert] = result.astype(jnp.bfloat16)

    for group in range(groups):
        place = slice(group * span, (group + 1) * span)
        rows = jnp.concatenate([packed_ref[expert, place] for expert in range(experts)], axis=0)
        summed = jnp.dot(placer_ref[group], rows, preferred_element_type=jnp.float32)
        tokens_ref[group, :, :width] = summed.astype(jnp.bfloat16)
        out_copy(group).start()
    for group in range(groups):
        out_copy(group).wait()


def run_experts(first, tokens, gate_up, down, block_rows, capacity):
    groups = len(tokens)
    tokens_n, wide = tokens[0].shape
    experts, _, units, width = gate_up.shape
    span = tokens_n // block_rows * capacity
    slots_n = experts * span
    anywhere = pl.BlockSpec(memory_space=pl.ANY)
    return pl.pallas_call(
        functools.partial(expert_kernel, (groups, block_rows, capacity)),
        in_specs=[pl.BlockSpec(memory_space=pltpu.SMEM)] + [anywhere] * (groups + 2),
        out_specs=[anywhere] * groups,
        out_shape=[jax.ShapeDtypeStruct((tokens_n, wide), jnp.bfloat16)] * groups,
        scratch_shapes=[
            pltpu.VMEM((groups, tokens_n, wide), jnp.bfloat16),
            pltpu.VMEM((2, 2, units, width), jnp.bfloat16),
            pltpu.VMEM((2, units, width), jnp.bfloat16),
            pltpu.VMEM((experts, groups * span, width), jnp.bfloat16),
            pltpu.VMEM((experts, groups * span, 128), jnp.float32),
            pltpu.VMEM((groups, tokens_n, slots_n), jnp.bfloat16),
            pltpu.SemaphoreType.DMA((groups,)),
            pltpu.SemaphoreType.DMA((2,)),
            pltpu.SemaphoreType.DMA((2,)),
            pltpu.SemaphoreType.DMA((groups,)),
        ],
        compiler_params=pltpu.CompilerParams(vmem_limit_bytes=46 << 20),
        cost_estimate=pl.CostEstimate(
            flops=6 * slots_n * groups * width * units,
            bytes_accessed=6 * experts * width * units,
            transcendentals=0,
        ),
    )(first, *tokens, gate_up, down)


def rms_scale(values, gain_vec):
    mean_sq = jnp.mean(values * values, axis=-1, keepdims=True)
    return values * lax.rsqrt(mean_sq + EPS) * gain_vec


def window_block(queries, key_rows, value_rows):
    scores = jnp.einsum(
        "qhgc,khc->hgqk", queries, key_rows, preferred_element_type=jnp.float32
    ) * HEAD_SIZE ** (-0.5)
    key_offset = jnp.arange(key_rows.shape[0])[None, :] - jnp.arange(queries.shape[0])[:, None]
    in_window = (key_offset >= 1) & (key_offset <= WINDOW_KEYS)
    scores = jnp.where(in_window, scores, -1e30)
    row_max = jnp.max(scores, axis=-1, keepdims=True)
    exponent = jnp.exp(scores - row_max)
    layer_weights = (exponent / jnp.sum(exponent, axis=-1, keepdims=True)).astype(jnp.bfloat16)
    attended = jnp.einsum(
        "hgqk,khc->qhgc", layer_weights, value_rows, preferred_element_type=jnp.float32
    )
    return attended.astype(jnp.bfloat16)


def local(
    stream_in,
    attn_gain,
    w_qkv,
    key_value_cache,
    w_out,
    mlp_gain,
    expert_index,
    gate_weight,
    w_gateup,
    w_down,
):
    seq_count = lax.axis_size("seq")
    tp_count = lax.axis_size("tp")
    length_local = stream_in.shape[0]
    heads_local = w_qkv.shape[1]
    query_group_width = QUERY_HEADS // KEY_VALUE_HEADS
    normed = rms_scale(stream_in.astype(jnp.float32), attn_gain).astype(jnp.bfloat16)
    projected_rows = jnp.einsum(
        "td,dhc->thc", normed, w_qkv, preferred_element_type=jnp.float32
    ).astype(jnp.bfloat16)
    projected_rows = projected_rows.reshape(
        length_local, heads_local, query_group_width + 2, HEAD_SIZE
    )
    queries = projected_rows[:, :, :query_group_width]
    kv_tail_rows = jnp.concatenate(
        [
            projected_rows[length_local - WINDOW_KEYS :, :, query_group_width],
            projected_rows[length_local - WINDOW_KEYS :, :, query_group_width + 1],
        ],
        axis=-1,
    )
    earlier = from_behind(kv_tail_rows, "seq", 1)
    at_start = lax.axis_index("seq") == 0
    earlier = jnp.where(at_start, key_value_cache, earlier)
    key_rows = jnp.concatenate(
        [earlier[:, :, :HEAD_SIZE], projected_rows[:, :, query_group_width]], axis=0
    )
    value_rows = jnp.concatenate(
        [earlier[:, :, HEAD_SIZE:], projected_rows[:, :, query_group_width + 1]], axis=0
    )
    attended = window_block(queries, key_rows, value_rows).reshape(
        length_local, heads_local * query_group_width * HEAD_SIZE
    )
    block_rows = length_local // tp_count
    plan = axis_plan(seq_count, tp_count)
    across = tp_count // 2

    terms = jnp.dot(attended, w_out, preferred_element_type=jnp.float32)
    terms = terms.reshape(across, 2, block_rows, MODEL_WIDTH)
    core = lax.axis_index("tp") % 2
    kept = lax.dynamic_index_in_dim(terms, core, 1, False)
    handed = lax.dynamic_index_in_dim(terms, 1 - core, 1, False).astype(jnp.bfloat16)
    kept = kept + swap(handed, 1, 1).astype(jnp.float32)
    place = lax.axis_index("tp") // 2
    attn_out = lax.dynamic_index_in_dim(kept, place, 0, False)
    for other in range(1, across):
        handed_on = lax.dynamic_index_in_dim(kept, place ^ other, 0, False).astype(jnp.bfloat16)
        attn_out = attn_out + swap(handed_on, 2 * other, 2 * other).astype(jnp.float32)
    own_start = lax.axis_index("tp") * block_rows
    residual = (
        lax.dynamic_slice_in_dim(stream_in, own_start, block_rows, 0).astype(jnp.float32) + attn_out
    )
    hidden_in = rms_scale(residual, mlp_gain).astype(jnp.bfloat16)

    experts_dev = w_gateup.shape[0]
    capacity = 2 * length_local * TOPK // (tp_count * EXPERTS)
    high = lax.reduce_precision(gate_weight, 8, 7)
    middle = lax.reduce_precision(gate_weight - high, 8, 7)
    low = lax.reduce_precision(gate_weight - high - middle, 8, 7)
    routing = jnp.concatenate([expert_index.astype(jnp.float32), high, middle, low], axis=1)
    routing = jnp.pad(routing, ((0, 0), (0, ROUTING - 4 * TOPK))).astype(jnp.bfloat16)
    gate_up = jnp.transpose(w_gateup, (0, 2, 3, 1))
    gate_up = pltpu.with_memory_space_constraint(gate_up, pltpu.HBM)
    down = pltpu.with_memory_space_constraint(w_down, pltpu.HBM)
    rows = jnp.concatenate([hidden_in, routing], axis=1)

    (slow, slow_step, _), inner = plan[0], plan[1:]
    (size, even, odd), (last_size, last_even, last_odd) = inner
    half = slow // 2

    def along(value, offset):
        return swap(value, offset * slow_step, offset * slow_step)

    others = [along(rows, offset) for offset in range(1, slow)]
    first_pieces, second_pieces = [rows] + others[: half - 1], others[half - 1 :]
    spread_a = [spread(rows, inner)]
    for piece in first_pieces[1:]:
        spread_a.append(spread(join([piece], 1, spread_a[0][1:2]), inner))
    forwards = [piece for pieces in spread_a for piece in pieces[1 : size + 1]]
    pair = join(second_pieces, 1, forwards + spread_a[0][size + 1 :])
    mine_a = join([piece for pieces in spread_a for piece in pieces])
    near = [swap(pair, other * even, other * odd) for other in range(1, size)]
    passed = [join([piece], 1, [mine_a]) for piece in near]
    pieces_b = [pair] + near
    for other in range(1, last_size):
        pieces_b += [
            swap(piece, other * last_even, other * last_odd) for piece in [pair] + passed
        ]
    mine_b = join(pieces_b, half)
    tokens = [mine_a, swap(mine_a, 1, 1), mine_b, swap(mine_b, 1, 1)]

    first = (lax.axis_index("seq") * experts_dev).astype(jnp.int32).reshape(1)
    sums = run_experts(first, tokens, gate_up, down, block_rows, capacity)

    last_kinds = [jnp.float32] + [jnp.bfloat16] * (last_size - 1)
    inner_kinds = [jnp.float32] + [jnp.bfloat16] * (size - 1)
    whole = [[kept, swap(handed, 1, 1)] for kept, handed in (sums[:2], sums[2:])]
    arrived = []
    after = []
    for offset in list(range(slow - 1, 0, -1)) + [0]:
        after = after + ([] if offset else arrived[:1])
        terms = fold(whole[offset // half], last_kinds, after, offset % half, half)
        terms = send_parts(terms, last_even, last_odd)
        after = terms[1:]
        behind = [] if offset else arrived[1:2]
        terms = send_parts(fold(terms, inner_kinds, behind), even, odd)
        if offset:
            arrived.append(along(fold(terms, [jnp.bfloat16])[0], offset))
        else:
            total = residual + fold(terms, [jnp.float32], arrived[-1:])[0][:, :MODEL_WIDTH]
    for part in arrived:
        total = total + part[:, :MODEL_WIDTH].astype(jnp.float32)
    return total.astype(jnp.bfloat16)


def solution(mesh):
    in_specs = (
        P("seq", None),
        P(),
        P(None, "tp", None),
        P(None, "tp", None),
        P("tp", None),
        P(),
        P(("seq", "tp"), None),
        P(("seq", "tp"), None),
        P("seq", None, None, "tp"),
        P("seq", "tp", None),
    )
    out_specs = P(("seq", "tp"), None)
    return jax.shard_map(local, mesh=mesh, in_specs=in_specs, out_specs=out_specs, check_vma=False)
```

```python
import functools

import jax
import jax.numpy as jnp
from jax import lax
from jax.experimental import pallas as pl
from jax.experimental.pallas import tpu as pltpu
from jax.sharding import PartitionSpec as P

MODEL_WIDTH = 2880
QUERY_HEADS = 64
KEY_VALUE_HEADS = 8
HEAD_SIZE = 64
WINDOW_KEYS = 128
EXPERTS = 32
TOPK = 4


EPS = 1e-05


def from_behind(value, axis, steps):
    count = lax.axis_size(axis)
    first, last = (max(0, -steps), min(count, count - steps))
    return lax.ppermute(value, axis, [(source, source + steps) for source in range(first, last)])


def axis_plan(seq_count, tp_count):
    across = tp_count // 2
    slow = min(4, seq_count)
    quick = seq_count // slow
    x_step, quick_step, slow_step = 2, 2 * across, 2 * across * quick
    along = [(slow, slow_step, slow_step)]
    if across == quick:
        along.append((across, x_step, quick_step))
        along.append((across, quick_step, x_step))
    else:
        along.append((across, x_step, x_step))
        along.append((quick, quick_step, quick_step))
    return along


def swap(value, even_mask, odd_mask):
    count = lax.axis_size("seq") * lax.axis_size("tp")
    pairs = [
        (device, device ^ (odd_mask if device % 2 else even_mask)) for device in range(count)
    ]
    return lax.ppermute(value, ("seq", "tp"), pairs)


def spread(piece, steps):
    pieces = [piece]
    for size, even, odd in steps:
        pieces = pieces + [
            swap(held, other * even, other * odd) for other in range(1, size) for held in pieces
        ]
    return pieces


ROUTING = 64
SMALL_KERNEL = 8 << 20


def join_kernel(count, pieces, *refs):
    parts, out_ref = refs[:count], refs[-1]
    rows = parts[0].shape[0] // pieces
    for piece in range(pieces):
        for place, part in enumerate(parts):
            start = (piece * count + place) * rows
            out_ref[start : start + rows, :] = part[piece * rows : (piece + 1) * rows, :]


def join(parts, pieces=1, after=()):
    rows, width = parts[0].shape
    return pl.pallas_call(
        functools.partial(join_kernel, len(parts), pieces),
        in_specs=[pl.BlockSpec(memory_space=pltpu.VMEM)] * len(parts)
        + [pl.BlockSpec(memory_space=pl.ANY)] * len(after),
        out_shape=jax.ShapeDtypeStruct((len(parts) * rows, width), parts[0].dtype),
        compiler_params=pltpu.CompilerParams(vmem_limit_bytes=SMALL_KERNEL),
        cost_estimate=pl.CostEstimate(
            flops=0, bytes_accessed=4 * len(parts) * rows * width, transcendentals=0
        ),
    )(*parts, *after)


def fold_kernel(count, outs_n, first_row, *refs):
    terms, outs = refs[:count], refs[len(refs) - outs_n :]
    rows = outs[0].shape[0]
    for place, out_ref in enumerate(outs):
        cut = slice(first_row + place * rows, first_row + (place + 1) * rows)
        total = terms[0][cut, :].astype(jnp.float32)
        for term in terms[1:]:
            total = total + term[cut, :].astype(jnp.float32)
        out_ref[...] = total.astype(out_ref.dtype)


def fold(terms, kinds, after=(), piece=0, pieces=1):
    rows, width = terms[0].shape
    rows = rows // (pieces * len(kinds))
    return pl.pallas_call(
        functools.partial(fold_kernel, len(terms), len(kinds), piece * len(kinds) * rows),
        in_specs=[pl.BlockSpec(memory_space=pltpu.VMEM)] * len(terms)
        + [pl.BlockSpec(memory_space=pl.ANY)] * len(after),
        out_shape=[jax.ShapeDtypeStruct((rows, width), kind) for kind in kinds],
        compiler_params=pltpu.CompilerParams(vmem_limit_bytes=SMALL_KERNEL),
        cost_estimate=pl.CostEstimate(
            flops=len(terms) * rows * len(kinds) * width,
            bytes_accessed=4 * len(terms) * rows * len(kinds) * width,
            transcendentals=0,
        ),
    )(*terms, *after)


def send_parts(parts, even, odd):
    return [parts[0]] + [
        swap(part, other * even, other * odd) for other, part in enumerate(parts[1:], 1)
    ]


def expert_kernel(sizes, first_ref, *refs):
    groups, block_rows, capacity = sizes
    ins = refs[:groups]
    gate_up_ref, down_ref = refs[groups : groups + 2]
    outs = refs[groups + 2 : 2 * groups + 2]
    tokens_ref, gate_up_buf, down_buf, packed_ref, gate_ref, placer_ref = refs[2 * groups + 2 : -4]
    token_sem, gate_up_sem, down_sem, out_sem = refs[-4:]
    experts, _, units, width = gate_up_ref.shape
    tokens_n = ins[0].shape[0]
    per_group = tokens_n // block_rows
    span = per_group * capacity
    slots_n = experts * span

    def token_copy(group):
        return pltpu.make_async_copy(ins[group], tokens_ref.at[group], token_sem.at[group])

    def out_copy(group):
        return pltpu.make_async_copy(tokens_ref.at[group], outs[group], out_sem.at[group])

    def gate_up_copy(expert):
        return pltpu.make_async_copy(
            gate_up_ref.at[expert], gate_up_buf.at[expert % 2], gate_up_sem.at[expert % 2]
        )

    def down_copy(expert):
        return pltpu.make_async_copy(
            down_ref.at[expert], down_buf.at[expert % 2], down_sem.at[expert % 2]
        )

    for group in range(groups):
        token_copy(group).start()
    gate_up_copy(0).start()
    down_copy(0).start()

    slot = lax.broadcasted_iota(jnp.int32, (slots_n, tokens_n), 0)
    token = lax.broadcasted_iota(jnp.int32, (slots_n, tokens_n), 1)
    expert_of = (slot // span + first_ref[0]).astype(jnp.float32)
    place_of = (slot % capacity).astype(jnp.float32)
    own_block = (slot // capacity) % per_group == token // block_rows
    before = lax.broadcasted_iota(jnp.int32, (tokens_n, tokens_n), 0)
    after = lax.broadcasted_iota(jnp.int32, (tokens_n, tokens_n), 1)
    earlier = (before // block_rows == after // block_rows) & (before < after)
    earlier = jnp.where(earlier, 1.0, 0.0).astype(jnp.bfloat16)
    start = width + ROUTING - 128
    for group in range(groups):
        token_copy(group).wait()
        tail = tokens_ref[group, :, start : start + 128].astype(jnp.float32)
        tail = jnp.transpose(tail)[128 - ROUTING :]
        member = jnp.zeros((slots_n, tokens_n), jnp.float32)
        gate = jnp.zeros((slots_n, tokens_n), jnp.float32)
        for choice in range(TOPK):
            hit = tail[choice : choice + 1] == expert_of
            weight = (
                tail[TOPK + choice : TOPK + choice + 1]
                + tail[2 * TOPK + choice : 2 * TOPK + choice + 1]
                + tail[3 * TOPK + choice : 3 * TOPK + choice + 1]
            )
            member = member + jnp.where(hit, 1.0, 0.0)
            gate = gate + jnp.where(hit, weight, 0.0)
        rank = jnp.dot(member.astype(jnp.bfloat16), earlier, preferred_element_type=jnp.float32)
        chosen = own_block & (rank == place_of) & (member > 0.5)
        hot = jnp.where(chosen, 1.0, 0.0)
        gate = jnp.sum(jnp.where(chosen, gate, 0.0), axis=1, keepdims=True)
        placer_ref[group] = jnp.transpose(hot).astype(jnp.bfloat16)
        rows = tokens_ref[group, :, :width]
        packed = jnp.dot(hot.astype(jnp.bfloat16), rows, preferred_element_type=jnp.float32)
        packed = packed.astype(jnp.bfloat16)
        for expert in range(experts):
            place = slice(group * span, (group + 1) * span)
            packed_ref[expert, place] = packed[expert * span : (expert + 1) * span]
            gate_ref[expert, place] = jnp.broadcast_to(
                gate[expert * span : (expert + 1) * span], (span, 128)
            )

    contract = (((1,), (1,)), ((), ()))
    for expert in range(experts):
        held = expert % 2
        if expert + 1 < experts:
            gate_up_copy(expert + 1).start()
            down_copy(expert + 1).start()
        gate_up_copy(expert).wait()
        rows = packed_ref[expert]
        both = lax.dot_general(
            rows,
            gate_up_buf[held].reshape(2 * units, width),
            contract,
            preferred_element_type=jnp.float32,
        )
        gate, up = both[:, :units], both[:, units:]
        act = gate / (1.0 + jnp.exp(-gate)) * up * gate_ref[expert][:, :1]
        act = act.astype(jnp.bfloat16)
        down_copy(expert).wait()
        result = jnp.dot(act, down_buf[held], preferred_element_type=jnp.float32)
        packed_ref[expert] = result.astype(jnp.bfloat16)

    for group in range(groups):
        place = slice(group * span, (group + 1) * span)
        rows = jnp.concatenate([packed_ref[expert, place] for expert in range(experts)], axis=0)
        summed = jnp.dot(placer_ref[group], rows, preferred_element_type=jnp.float32)
        tokens_ref[group, :, :width] = summed.astype(jnp.bfloat16)
        out_copy(group).start()
    for group in range(groups):
        out_copy(group).wait()


def run_experts(first, tokens, gate_up, down, block_rows, capacity):
    groups = len(tokens)
    tokens_n, wide = tokens[0].shape
    experts, _, units, width = gate_up.shape
    span = tokens_n // block_rows * capacity
    slots_n = experts * span
    anywhere = pl.BlockSpec(memory_space=pl.ANY)
    return pl.pallas_call(
        functools.partial(expert_kernel, (groups, block_rows, capacity)),
        in_specs=[pl.BlockSpec(memory_space=pltpu.SMEM)] + [anywhere] * (groups + 2),
        out_specs=[anywhere] * groups,
        out_shape=[jax.ShapeDtypeStruct((tokens_n, wide), jnp.bfloat16)] * groups,
        scratch_shapes=[
            pltpu.VMEM((groups, tokens_n, wide), jnp.bfloat16),
            pltpu.VMEM((2, 2, units, width), jnp.bfloat16),
            pltpu.VMEM((2, units, width), jnp.bfloat16),
            pltpu.VMEM((experts, groups * span, width), jnp.bfloat16),
            pltpu.VMEM((experts, groups * span, 128), jnp.float32),
            pltpu.VMEM((groups, tokens_n, slots_n), jnp.bfloat16),
            pltpu.SemaphoreType.DMA((groups,)),
            pltpu.SemaphoreType.DMA((2,)),
            pltpu.SemaphoreType.DMA((2,)),
            pltpu.SemaphoreType.DMA((groups,)),
        ],
        compiler_params=pltpu.CompilerParams(vmem_limit_bytes=46 << 20),
        cost_estimate=pl.CostEstimate(
            flops=6 * slots_n * groups * width * units,
            bytes_accessed=6 * experts * width * units,
            transcendentals=0,
        ),
    )(first, *tokens, gate_up, down)


def rms_scale(values, gain_vec):
    mean_sq = jnp.mean(values * values, axis=-1, keepdims=True)
    return values * lax.rsqrt(mean_sq + EPS) * gain_vec


def window_block(queries, key_rows, value_rows):
    scores = jnp.einsum(
        "qhgc,khc->hgqk", queries, key_rows, preferred_element_type=jnp.float32
    ) * HEAD_SIZE ** (-0.5)
    key_offset = jnp.arange(key_rows.shape[0])[None, :] - jnp.arange(queries.shape[0])[:, None]
    in_window = (key_offset >= 1) & (key_offset <= WINDOW_KEYS)
    scores = jnp.where(in_window, scores, -1e30)
    row_max = jnp.max(scores, axis=-1, keepdims=True)
    exponent = jnp.exp(scores - row_max)
    layer_weights = (exponent / jnp.sum(exponent, axis=-1, keepdims=True)).astype(jnp.bfloat16)
    attended = jnp.einsum(
        "hgqk,khc->qhgc", layer_weights, value_rows, preferred_element_type=jnp.float32
    )
    return attended.astype(jnp.bfloat16)


def local(
    stream_in,
    attn_gain,
    w_qkv,
    key_value_cache,
    w_out,
    mlp_gain,
    expert_index,
    gate_weight,
    w_gateup,
    w_down,
):
    seq_count = lax.axis_size("seq")
    tp_count = lax.axis_size("tp")
    length_local = stream_in.shape[0]
    heads_local = w_qkv.shape[1]
    query_group_width = QUERY_HEADS // KEY_VALUE_HEADS
    normed = rms_scale(stream_in.astype(jnp.float32), attn_gain).astype(jnp.bfloat16)
    projected_rows = jnp.einsum(
        "td,dhc->thc", normed, w_qkv, preferred_element_type=jnp.float32
    ).astype(jnp.bfloat16)
    projected_rows = projected_rows.reshape(
        length_local, heads_local, query_group_width + 2, HEAD_SIZE
    )
    queries = projected_rows[:, :, :query_group_width]
    kv_tail_rows = jnp.concatenate(
        [
            projected_rows[length_local - WINDOW_KEYS :, :, query_group_width],
            projected_rows[length_local - WINDOW_KEYS :, :, query_group_width + 1],
        ],
        axis=-1,
    )
    earlier = from_behind(kv_tail_rows, "seq", 1)
    at_start = lax.axis_index("seq") == 0
    earlier = jnp.where(at_start, key_value_cache, earlier)
    key_rows = jnp.concatenate(
        [earlier[:, :, :HEAD_SIZE], projected_rows[:, :, query_group_width]], axis=0
    )
    value_rows = jnp.concatenate(
        [earlier[:, :, HEAD_SIZE:], projected_rows[:, :, query_group_width + 1]], axis=0
    )
    attended = window_block(queries, key_rows, value_rows).reshape(
        length_local, heads_local * query_group_width * HEAD_SIZE
    )
    block_rows = length_local // tp_count
    plan = axis_plan(seq_count, tp_count)
    across = tp_count // 2

    terms = jnp.dot(attended, w_out, preferred_element_type=jnp.float32)
    terms = terms.reshape(across, 2, block_rows, MODEL_WIDTH)
    core = lax.axis_index("tp") % 2
    kept = lax.dynamic_index_in_dim(terms, core, 1, False)
    handed = lax.dynamic_index_in_dim(terms, 1 - core, 1, False).astype(jnp.bfloat16)
    kept = kept + swap(handed, 1, 1).astype(jnp.float32)
    place = lax.axis_index("tp") // 2
    attn_out = lax.dynamic_index_in_dim(kept, place, 0, False)
    for other in range(1, across):
        handed_on = lax.dynamic_index_in_dim(kept, place ^ other, 0, False).astype(jnp.bfloat16)
        attn_out = attn_out + swap(handed_on, 2 * other, 2 * other).astype(jnp.float32)
    own_start = lax.axis_index("tp") * block_rows
    residual = (
        lax.dynamic_slice_in_dim(stream_in, own_start, block_rows, 0).astype(jnp.float32) + attn_out
    )
    hidden_in = rms_scale(residual, mlp_gain).astype(jnp.bfloat16)

    experts_dev = w_gateup.shape[0]
    capacity = 2 * length_local * TOPK // (tp_count * EXPERTS)
    high = lax.reduce_precision(gate_weight, 8, 7)
    middle = lax.reduce_precision(gate_weight - high, 8, 7)
    low = lax.reduce_precision(gate_weight - high - middle, 8, 7)
    routing = jnp.concatenate([expert_index.astype(jnp.float32), high, middle, low], axis=1)
    routing = jnp.pad(routing, ((0, 0), (0, ROUTING - 4 * TOPK))).astype(jnp.bfloat16)
    gate_up = jnp.transpose(w_gateup, (0, 2, 3, 1))
    gate_up = pltpu.with_memory_space_constraint(gate_up, pltpu.HBM)
    down = pltpu.with_memory_space_constraint(w_down, pltpu.HBM)
    rows = jnp.concatenate([hidden_in, routing], axis=1)

    (slow, slow_step, _), inner = plan[0], plan[1:]
    (size, even, odd), (last_size, last_even, last_odd) = inner
    half = slow // 2

    def along(value, offset):
        return swap(value, offset * slow_step, offset * slow_step)

    others = [along(rows, offset) for offset in range(1, slow)]
    first_pieces, second_pieces = [rows] + others[: half - 1], others[half - 1 :]
    spread_a = [spread(rows, inner)]
    for piece in first_pieces[1:]:
        spread_a.append(spread(join([piece], 1, spread_a[0][1:2]), inner))
    forwards = [piece for pieces in spread_a for piece in pieces[1 : size + 1]]
    pair = join(second_pieces, 1, forwards + spread_a[0][size + 1 :])
    mine_a = join([piece for pieces in spread_a for piece in pieces])
    near = [swap(pair, other * even, other * odd) for other in range(1, size)]
    passed = [join([piece], 1, [mine_a]) for piece in near]
    pieces_b = [pair] + near
    for other in range(1, last_size):
        pieces_b += [
            swap(piece, other * last_even, other * last_odd) for piece in [pair] + passed
        ]
    mine_b = join(pieces_b, half)
    tokens = [mine_a, swap(mine_a, 1, 1), mine_b, swap(mine_b, 1, 1)]

    first = (lax.axis_index("seq") * experts_dev).astype(jnp.int32).reshape(1)
    sums = run_experts(first, tokens, gate_up, down, block_rows, capacity)

    last_kinds = [jnp.float32] + [jnp.bfloat16] * (last_size - 1)
    inner_kinds = [jnp.float32] + [jnp.bfloat16] * (size - 1)
    whole = [[kept, swap(handed, 1, 1)] for kept, handed in (sums[:2], sums[2:])]
    arrived = []
    after = []
    for offset in list(range(slow - 1, 0, -1)) + [0]:
        after = after + ([] if offset else arrived[:1])
        terms = fold(whole[offset // half], last_kinds, after, offset % half, half)
        terms = send_parts(terms, last_even, last_odd)
        after = terms[1:]
        terms = send_parts(fold(terms, inner_kinds), even, odd)
        if offset:
            arrived.append(along(fold(terms, [jnp.bfloat16])[0], offset))
        else:
            total = residual + fold(terms, [jnp.float32], arrived[1:])[0][:, :MODEL_WIDTH]
    for part in arrived:
        total = total + part[:, :MODEL_WIDTH].astype(jnp.float32)
    return total.astype(jnp.bfloat16)


def solution(mesh):
    in_specs = (
        P("seq", None),
        P(),
        P(None, "tp", None),
        P(None, "tp", None),
        P("tp", None),
        P(),
        P(("seq", "tp"), None),
        P(("seq", "tp"), None),
        P("seq", None, None, "tp"),
        P("seq", "tp", None),
    )
    out_specs = P(("seq", "tp"), None)
    return jax.shard_map(local, mesh=mesh, in_specs=in_specs, out_specs=out_specs, check_vma=False)
```
